256 devices in a mesh: grp: 4 (over y), dev: 64 (over x, z, core).
Axes of the slice: x: 4, y: 4, z: 8, core: 2. Of those that a mesh axis runs over, the one named last changes fastest.
Arguments:
- features: bfloat16 [32768, 768], P(('grp', 'dev')), may hold values from -6 to 6
- neighbours: int32 [32768, 25], P(('grp', 'dev')), may hold values from 0 to 32767, as said below
- neighbour_mask: int32 [32768, 25], P(('grp', 'dev')), may hold values from 0 to 1, as said below
- layer2_position: int32 [32768], P(('grp', 'dev')), may hold values from 0 to 32767, as said below
- self_weight1: bfloat16 [768, 1024], replicated, may hold values from -0.21875 to 0.21875
- neigh_weight1: bfloat16 [768, 1024], replicated, may hold values from -0.4375 to 0.4375
- self_weight2: bfloat16 [1024, 1024], replicated, may hold values from -0.1875 to 0.1875
- neigh_weight2: bfloat16 [1024, 1024], replicated, may hold values from -0.375 to 0.375
Outputs:
- embeddings: bfloat16 [32768, 1024], P(('grp', 'dev'))
The draws below stay inside these ranges and needn't reach their ends.
Inputs may be any that keep to these rules, and one draw needn't show every extreme that they name: `neighbours`: node n is owned by device n // 128 (devices numbered grp-major). Slot 0 of every node is valid. Of one device's nodes, at most 6 valid slots name nodes of any one other device, and exactly 6 do for some other device; 765 slots of one device name other devices' nodes, all of them valid. Invalid slots hold ids of the device's own nodes. `neighbour_mask`: values 0 or 1; 1 at slot 0 and wherever the neighbour lies on another device. A permutation of the nodes; a node's new owner, layer2_position // 128, is in the same group as its old one. One device hands exactly 4 nodes to each owner of its group whose index within the group differs from its own by an even number, and none to the others.
All inputs are finite; a program needn't handle non-finite values.
Results may differ from the reference program's by a relative error of at most 0.0052.
Values may be sent and summed in bfloat16 or wider, within the bound.
A program may use at most 64 MiB of HBM per device.

```python
import jax
import jax.numpy as jnp
from jax import lax

F_IN = 768
HID = 1024
DEG = 25
ROWS = 128
CAP = 6
REMOTE = 765
CAP2 = 4
NODES = 32768
N_GRP = 4
N_DEV = 64


def edge_plan(key):
    device_count = N_GRP * N_DEV
    edge_count = ROWS * DEG

    def one_device(device_index):
        device_key = jax.random.fold_in(key, device_index)
        key_list = jax.random.split(device_key, 7)
        offsets = jnp.repeat(jnp.arange(1, device_count, dtype=jnp.int32), CAP)
        mixed = jax.random.permutation(key_list[0], offsets)
        forced = jax.random.randint(key_list[1], (), 1, device_count)
        ordering = jnp.argsort((mixed != forced).astype(jnp.int32), stable=True)
        chosen = mixed[ordering][:REMOTE]
        owners = (device_index + chosen) % device_count
        remote_ids = owners * ROWS + jax.random.randint(key_list[2], (REMOTE,), 0, ROWS)
        local_ids = device_index * ROWS + jax.random.randint(key_list[3], (edge_count,), 0, ROWS)
        places = jax.random.permutation(key_list[4], edge_count)[:REMOTE]
        neighbour_ids = local_ids.at[places].set(remote_ids)
        remote_flag = jnp.zeros((edge_count,), jnp.int32).at[places].set(1)
        keep_level = jax.random.randint(key_list[5], (), 3, 10)
        coin_flips = jax.random.randint(key_list[6], (edge_count,), 0, 10)
        leading = jnp.arange(edge_count) % DEG == 0
        usable = (coin_flips < keep_level) | (remote_flag == 1) | leading
        return (neighbour_ids.astype(jnp.int32), jnp.where(usable, 1, 0).astype(jnp.int32))
    neighbour_ids, usable = jax.vmap(one_device)(jnp.arange(device_count, dtype=jnp.int32))
    return (neighbour_ids.reshape(NODES, DEG), usable.reshape(NODES, DEG))


def draw_neighbours(key, part):
    return edge_plan(jax.random.fold_in(key, 11))[0]


def draw_neighbour_mask(key, part):
    return edge_plan(jax.random.fold_in(key, 11))[1]


def draw_layer2_position(key, part):
    block_total = N_DEV // 2

    def one_group(group_index):
        group_key = jax.random.fold_in(key, group_index)
        key_list = jax.random.split(group_key, 3)
        offsets = 2 * jax.random.permutation(key_list[0], block_total).astype(jnp.int32)
        sender_order = jax.vmap(lambda single: jax.random.permutation(single, ROWS))(jax.random.split(key_list[1], N_DEV))
        target_order = jax.vmap(lambda single: jax.random.permutation(single, ROWS))(jax.random.split(key_list[2], N_DEV))
        slot_index = jnp.arange(ROWS, dtype=jnp.int32)
        block_ids = slot_index // CAP2
        receiver = (jnp.arange(N_DEV, dtype=jnp.int32)[:, None] + offsets[block_ids][None, :]) % N_DEV
        position = (group_index * N_DEV + receiver) * ROWS + target_order[receiver, slot_index[None, :]]
        sender_rows = jnp.arange(N_DEV, dtype=jnp.int32)[:, None]
        return jnp.zeros((N_DEV, ROWS), jnp.int32).at[sender_rows, sender_order].set(position.astype(jnp.int32))
    return jax.vmap(one_group)(jnp.arange(N_GRP, dtype=jnp.int32)).reshape(NODES)


def block_scale(key, extent, shards, least, high):
    def one(dim, blocks):
        heights = jax.random.uniform(jax.random.fold_in(jax.random.fold_in(key, 6), dim), (blocks,), jnp.float32, least / len(shards), high / len(shards))
        return jnp.repeat(jnp.exp(heights), extent[dim] // blocks).reshape((-1,) + (1,) * (len(extent) - dim - 1))

    factor_of = one(*shards[0])
    for cut in shards[1:]:
        factor_of = factor_of * one(*cut)
    return factor_of


def scatter_about(stream_key, extent, scale, bound, pieces=(), kind=jnp.bfloat16):
    values = jax.random.normal(stream_key, extent, jnp.float32) * scale
    if len(pieces) > 0:
        values = block_scale(stream_key, extent, pieces, -0.22, 0.18) * values
    return jnp.clip(values, min=-bound, max=bound).astype(kind)


def setup_inputs(seed: int = 0) -> dict:
    seeds = jax.random.split(jax.random.key(seed), 9)
    return {
        "features": scatter_about(seeds[0], (NODES, F_IN), 1.0, 6.0, ((0, 256),)),
        "neighbours": draw_neighbours(jax.random.fold_in(seeds[8], 71), 0),
        "neighbour_mask": draw_neighbour_mask(jax.random.fold_in(seeds[8], 71), 0),
        "layer2_position": draw_layer2_position(jax.random.fold_in(seeds[8], 71), 0),
        "self_weight1": scatter_about(seeds[4], (F_IN, HID), F_IN ** -0.5, 0.21875),
        "neigh_weight1": scatter_about(seeds[5], (F_IN, HID), (F_IN // 4) ** -0.5, 0.4375),
        "self_weight2": scatter_about(seeds[6], (HID, HID), HID ** -0.5, 0.1875),
        "neigh_weight2": scatter_about(seeds[7], (HID, HID), (HID // 4) ** -0.5, 0.375),
    }


def aggregate_layer(table, self_rows, neighbours, neighbour_mask, self_weight, neigh_weight):
    device_count = neighbours.shape[0] // ROWS
    ids_blocks = neighbours.reshape(device_count, ROWS, DEG)
    mask_blocks = neighbour_mask.reshape(device_count, ROWS, DEG)
    self_blocks = self_rows.reshape(device_count, ROWS, self_rows.shape[1])

    def one_block(packed):
        block_ids, block_mask, block_self = packed
        picked = table[block_ids].astype(jnp.float32)
        weights = block_mask.astype(jnp.float32)
        summed = jnp.sum(picked * weights[:, :, None], axis=1)
        degree_count = jnp.sum(weights, axis=1)
        mean_rows = (summed / degree_count[:, None]).astype(jnp.bfloat16)
        return jnp.dot(block_self, self_weight, preferred_element_type=jnp.float32) + jnp.dot(mean_rows, neigh_weight, preferred_element_type=jnp.float32)

    result = lax.map(one_block, (ids_blocks, mask_blocks, self_blocks))
    return result.reshape(-1, self_weight.shape[1])


def reference(features, neighbours, neighbour_mask, layer2_position, self_weight1, neigh_weight1, self_weight2, neigh_weight2):
    hidden = jax.nn.relu(aggregate_layer(features, features, neighbours, neighbour_mask, self_weight1, neigh_weight1)).astype(jnp.bfloat16)
    final = aggregate_layer(hidden, hidden, neighbours, neighbour_mask, self_weight2, neigh_weight2).astype(jnp.bfloat16)
    embeddings = jnp.zeros_like(final).at[layer2_position.astype(jnp.int32)].set(final)
    return embeddings
```

```python
import jax
import jax.numpy as jnp
from jax import lax
from jax.experimental import pallas as pl
from jax.experimental.pallas import tpu as pltpu
from jax.sharding import PartitionSpec as P

NX, NZ, NC = 4, 8, 2
CAP = 6
CHUNK = 256
LANES = 128
BF = jnp.bfloat16
F32 = jnp.float32
MESH = pl.DeviceIdType.MESH


def iota(shape, dim):
    return lax.broadcasted_iota(jnp.int32, shape, dim)


def mm(a, b):
    return jnp.dot(a, b, preferred_element_type=F32)


def one_zero(cond):
    return jnp.where(cond, 1.0, 0.0).astype(BF)


def kernel(
    nb_ref,
    mk_ref,
    pos_ref,
    feat_hbm,
    ws1_hbm,
    wn1_hbm,
    ws2_hbm,
    wn2_hbm,
    out_ref,
    ws1,
    wn1,
    ws2,
    wn2,
    table,
    serve,
    ans,
    pick,
    key_ref,
    adj,
    adj2,
    loc,
    loc2,
    cnt,
    cnt2,
    slot_p,
    slot_id,
    slot_row,
    lists,
    asked,
    acc,
    hid,
    xbuf,
    arrx,
    zbuf,
    arrz,
    load_sem,
    ring_send,
    ring_recv,
    req_send,
    req_recv,
    ans_send,
    ans_recv,
    x_send,
    x_recv,
    z_send,
    z_recv,
):
    rows, degree = nb_ref.shape
    ny = lax.axis_size("grp")
    n_dev = NX * NZ * NC
    ncol = NX * ny * NC
    block = CAP * NZ
    chunk = table.shape[2]
    n1 = feat_hbm.shape[1] // chunk
    n2 = wn2.shape[0] // chunk
    hidden_width = wn2.shape[0]
    half = NZ // 2
    rank2 = rows // (NX * NZ)
    me_y = lax.axis_index("grp")
    me_dev = lax.axis_index("dev")
    me_x = me_dev // (NZ * NC)
    me_z = me_dev // NC % NZ
    me_c = me_dev % NC

    def at(x, y, z, c):
        return (y, (x * NZ + z) * NC + c)

    def ahead(d):
        return at(
            (me_x + d // (ny * NC)) % NX,
            (me_y + d // NC % ny) % ny,
            me_z,
            (me_c + d % NC) % NC,
        )

    def behind(d):
        return at(
            (me_x + NX - d // (ny * NC)) % NX,
            (me_y + ny - d // NC % ny) % ny,
            me_z,
            (me_c + NC - d % NC) % NC,
        )

    def along_z(dz):
        return at(me_x, me_y, (me_z + dz) % NZ, me_c)

    def along_x(dx):
        return at((me_x + dx) % NX, me_y, me_z, me_c)

    def drain(ref, sem):
        pltpu.make_async_copy(ref, ref, sem).wait()

    own = pl.ds(pl.multiple_of(me_z * rows, rows), rows)

    loads = []
    for k in range(n1):
        loads.append(
            pltpu.make_async_copy(
                feat_hbm.at[:, pl.ds(k * chunk, chunk)], table.at[k, own], load_sem.at[k]
            )
        )
    for k, (far, near) in enumerate(
        ((ws1_hbm, ws1), (wn1_hbm, wn1), (ws2_hbm, ws2), (wn2_hbm, wn2))
    ):
        loads.append(pltpu.make_async_copy(far, near, load_sem.at[n1 + k]))
    for load in loads:
        load.start()

    barrier = pltpu.get_barrier_semaphore()

    @pl.loop(1, NZ)
    def _(dz):
        pl.semaphore_signal(barrier, inc=1, device_id=along_z(dz), device_id_type=MESH)

    @pl.loop(1, ncol)
    def _(d):
        pl.semaphore_signal(barrier, inc=1, device_id=ahead(d), device_id_type=MESH)

    pl.semaphore_wait(barrier, NZ - 1 + ncol - 1)

    def ring_block(k, s, way, last):
        from_z = (me_z + NZ - (s - 1)) % NZ if way == 0 else (me_z + s - 1) % NZ
        if last:
            start = from_z * rows + way * (rows // 2)
            return table.at[k, pl.ds(pl.multiple_of(start, rows // 2), rows // 2)]
        return table.at[k, pl.ds(pl.multiple_of(from_z * rows, rows), rows)]

    def ring_copy(k, s, way, last):
        ref = ring_block(k, s, way, last)
        return pltpu.make_async_remote_copy(
            src_ref=ref,
            dst_ref=ref,
            send_sem=ring_send.at[k, way, s - 1],
            recv_sem=ring_recv.at[k, way, s - 1],
            device_id=along_z(1 if way == 0 else NZ - 1),
            device_id_type=MESH,
        )

    def ring_step(k, s):
        for way in range(2):

            @pl.when(s > 1)
            def _():
                drain(ring_block(k, s, way, False), ring_recv.at[k, way, s - 2])

            @pl.when(s < half)
            def _():
                ring_copy(k, s, way, False).start()

            @pl.when(s == half)
            def _():
                ring_copy(k, s, way, True).start()

    def ring_end(k):
        for way in range(2):
            drain(ring_block(k, half + 1, way, True), ring_recv.at[k, way, half - 1])

    for k in range(n1):
        loads[k].wait()
    ring_step(0, 1)

    nb = nb_ref[...]
    mk = mk_ref[...]
    owner = nb // rows
    row = nb % rows
    o_y = owner // n_dev
    o_dev = owner % n_dev
    o_x = o_dev // (NZ * NC)
    o_z = o_dev // NC % NZ
    o_c = o_dev % NC
    mine = owner == me_y * n_dev + me_dev
    valid = mk > 0
    remote = valid & jnp.logical_not(mine)
    col = (
        ((me_x + NX - o_x) % NX) * (ny * NC)
        + ((me_y + ny - o_y) % ny) * NC
        + (me_c + NC - o_c) % NC
    )
    col = jnp.where(remote, col, -4096)
    slot_id[...] = o_z * rows + row + 1
    slot_row[...] = jnp.where(valid & mine, row, -1)
    count = jnp.sum(mk.astype(F32), axis=1, keepdims=True)
    cnt[...] = jnp.broadcast_to(count, (rows, LANES))

    pack = LANES // ncol
    lane = iota((rows, LANES), 1)
    sub = iota((rows, LANES), 0)
    lower = one_zero(lane < sub)
    ones = jnp.ones((rows, LANES), BF)
    same = lane % ncol == sub % ncol
    every = one_zero(same)
    before = one_zero(same & (sub // ncol < lane // ncol))
    so_far = jnp.zeros((rows, LANES), F32)
    cols = []
    for j in range(0, degree, pack):
        members = range(j, min(j + pack, degree))
        hot = jnp.zeros((rows, LANES), jnp.bool_)
        for s in members:
            hot = hot | (col[:, s : s + 1] == lane - (s - j) * ncol)
        hot = one_zero(hot)
        totals = mm(ones, hot)
        rank = (
            mm(lower, hot)
            + mm(totals.astype(BF), before)
            + mm(so_far.astype(BF), every)
        )
        so_far = so_far + totals
        rank = rank * hot.astype(F32)
        for s in members:
            group = lane // ncol == s - j
            cols.append(jnp.sum(jnp.where(group, rank, 0.0), axis=1, keepdims=True))
    lane_s = iota((rows, degree), 1)
    ranks = jnp.zeros((rows, degree), F32)
    for s in range(degree):
        ranks = jnp.where(lane_s == s, cols[s], ranks)
    slot_p[...] = jnp.where(remote, col * block + ranks.astype(jnp.int32), -1)

    ring_step(0, 2)

    tiles = ncol * block // LANES
    lists[...] = jnp.zeros_like(lists)

    @pl.loop(0, rows // 8)
    def _(i):
        at_rows = pl.ds(pl.multiple_of(i * 8, 8), 8)
        p8 = slot_p[at_rows, :]
        id8 = slot_id[at_rows, :]
        row8 = slot_row[at_rows, :]
        lane8 = iota((8, LANES), 1)
        p_all = [jnp.broadcast_to(p8[:, s : s + 1], (8, LANES)) for s in range(degree)]
        id_all = [jnp.broadcast_to(id8[:, s : s + 1], (8, LANES)) for s in range(degree)]
        for t in range(tiles):
            got = jnp.zeros((8, LANES), jnp.int32)
            for s in range(degree):
                got = jnp.where(p_all[s] == lane8 + t * LANES, id_all[s], got)
            key_ref[at_rows, t * LANES : (t + 1) * LANES] = got
            lists[t] = lists[t] + jnp.sum(got, axis=0, keepdims=True)
        near = jnp.zeros((8, LANES), F32)
        for s in range(degree):
            near = near + jnp.where(row8[:, s : s + 1] == lane8, 1.0, 0.0)
        loc[at_rows, :] = near

    window = 8 * block // LANES

    def request(d):
        return pltpu.make_async_remote_copy(
            src_ref=lists.at[pl.ds(d // 8 * window, window)],
            dst_ref=asked.at[d],
            send_sem=req_send,
            recv_sem=req_recv,
            device_id=behind(d),
            device_id_type=MESH,
        )

    @pl.loop(1, ncol)
    def _(d):
        request(d).start()

    asked[0] = lists[0:window]
    ring_step(0, 3)

    pos = pos_ref[...]
    t_dev = pos // rows % n_dev
    t_x = t_dev // (NZ * NC)
    t_z = t_dev // NC % NZ
    target = ((t_x + NX - me_x) % NX) * NZ + (t_z + NZ - me_z) % NZ
    hot_t = iota((NX * NZ, rows), 0) == target
    ahead_of = mm(one_zero(hot_t), one_zero(sub < lane))
    rank_t = jnp.sum(jnp.where(hot_t, ahead_of, 0.0), axis=0, keepdims=True)
    place = target * rank2 + rank_t.astype(jnp.int32)
    order = place == sub
    move = one_zero(order)
    pos_b = mm(jnp.where(order, (pos % rows).astype(F32), 0.0).astype(BF), ones)
    xbuf[:, :, hidden_width:] = pos_b.astype(BF).reshape(NX, NZ * rank2, LANES)
    adj[...] = one_zero(key_ref[...] > 0)
    adj2[...] = mm(move, adj[...]).astype(BF)
    loc2[...] = mm(move, loc[...].astype(BF))
    cnt2[...] = mm(move, cnt[...].astype(BF))
    ring_step(0, 4)

    drain(asked.at[pl.ds(1, ncol - 1)], req_recv)

    @pl.loop(0, ncol)
    def _(d):
        got = asked[d]
        place = iota((block, LANES), 0) + d % 8 * block
        found = jnp.zeros((block, LANES), jnp.int32)
        for t in range(window):
            piece = jnp.broadcast_to(got[t], (block, LANES))
            found = found + jnp.where(iota((block, LANES), 1) + t * LANES == place, piece, 0)
        found = jnp.sum(found, axis=1, keepdims=True)
        hit = iota((block, NZ * rows), 1) + 1 == found
        pick[pl.ds(pl.multiple_of(d * block, block), block), :] = one_zero(hit)

    ring_end(0)

    group = 8

    def reply(k, d):
        return pltpu.make_async_remote_copy(
            src_ref=serve.at[k, d],
            dst_ref=ans.at[k, d],
            send_sem=ans_send.at[k],
            recv_sem=ans_recv.at[k],
            device_id=ahead(d),
            device_id_type=MESH,
        )

    def serve_all(first, last):
        @pl.loop(first, last)
        def _(k):
            @pl.loop(0, ncol // group)
            def _(j):
                some = pl.ds(pl.multiple_of(j * group * block, group * block), group * block)
                picked = mm(pick[some, :], table[k]).astype(BF)
                serve[k, pl.ds(j * group, group)] = picked.reshape(group, block, chunk)

                @pl.loop(0, group)
                def _(i):
                    d = j * group + i

                    @pl.when(d > 0)
                    def _():
                        reply(k, d).start()

                @pl.when(k + 1 < last)
                def _():
                    for s in range(1, half + 1):

                        @pl.when(j == (s - 1) * (ncol // group) // half)
                        def _():
                            ring_step(k + 1, s)

            ans[k, 0] = serve[k, 0]

            @pl.when(k + 1 < last)
            def _():
                ring_end(k + 1)

    def mean(k, adjacency, near, rows_own, degrees):
        drain(ans.at[k, pl.ds(1, ncol - 1)], ans_recv.at[k])
        summed = mm(adjacency[...], ans[k].reshape(ncol * block, chunk)) + mm(
            near[...].astype(BF), rows_own
        )
        return (summed / degrees[:, 0:1]).astype(BF)

    def part(k):
        return slice(k * chunk, (k + 1) * chunk)

    serve_all(0, n1)
    loads[n1].wait()
    loads[n1 + 1].wait()
    for n in range(n2):
        total = mm(table[0, own, :], ws1[part(0), part(n)])
        for k in range(1, n1):
            total = total + mm(table[k, own, :], ws1[part(k), part(n)])
        acc[:, part(n)] = total
    for k in range(n1 - 1):
        m = mean(k, adj, loc, table[k, own, :], cnt)
        for n in range(n2):
            acc[:, part(n)] += mm(m, wn1[part(k), part(n)])
    m = mean(n1 - 1, adj, loc, table[n1 - 1, own, :], cnt)
    for n in range(n2):
        total = acc[:, part(n)] + mm(m, wn1[part(n1 - 1), part(n)])
        table[n1 + n, own, :] = jnp.maximum(total, 0.0).astype(BF)
        if n == 0:
            ring_step(n1, 1)
    for s in range(2, half + 1):
        ring_step(n1, s)
    for n in range(n2):
        hid[:, part(n)] = mm(move, table[n1 + n, own, :]).astype(BF)
    ring_end(n1)
    serve_all(n1, n1 + n2)
    loads[n1 + 2].wait()
    loads[n1 + 3].wait()
    for n in range(n2):
        acc[:, part(n)] = mm(hid[...], ws2[:, part(n)])
    for k in range(n2):
        m = mean(n1 + k, adj2, loc2, table[n1 + k, own, :], cnt2)
        for n in range(n2):
            acc[:, part(n)] += mm(m, wn2[part(k), part(n)])
    xbuf[:, :, :hidden_width] = acc[...].astype(BF).reshape(NX, NZ * rank2, hidden_width)

    def x_copy(dx):
        return pltpu.make_async_remote_copy(
            src_ref=xbuf.at[dx],
            dst_ref=arrx.at[dx],
            send_sem=x_send,
            recv_sem=x_recv,
            device_id=along_x(dx),
            device_id_type=MESH,
        )

    def z_copy(dz):
        return pltpu.make_async_remote_copy(
            src_ref=zbuf.at[dz],
            dst_ref=arrz.at[dz],
            send_sem=z_send,
            recv_sem=z_recv,
            device_id=along_z(dz),
            device_id_type=MESH,
        )

    @pl.loop(1, NX)
    def _(dx):
        x_copy(dx).start()

    arrx[0] = xbuf[0]
    drain(arrx.at[pl.ds(1, NX - 1)], x_recv)
    width = hidden_width + LANES
    source = (
        sub // rank2 % NX * (NZ * rank2) + sub // (NX * rank2) * rank2 + sub % rank2
    )
    turned = mm(one_zero(source == lane), arrx[...].reshape(rows, width)).astype(BF)
    zbuf[...] = turned.reshape(NZ, NX * rank2, width)

    @pl.loop(1, NZ)
    def _(dz):
        z_copy(dz).start()

    arrz[0] = zbuf[0]
    drain(arrz.at[pl.ds(1, NZ - 1)], z_recv)
    landed = arrz[...].reshape(rows, width)
    put = one_zero(landed[:, hidden_width:].astype(F32) == lane.astype(F32))
    out_ref[...] = lax.dot_general(
        put,
        landed[:, :hidden_width],
        (((0,), (0,)), ((), ())),
        preferred_element_type=F32,
    ).astype(BF)

    drain(lists_all(asked, ncol), req_send)
    drain(xbuf.at[pl.ds(1, NX - 1)], x_send)
    drain(zbuf.at[pl.ds(1, NZ - 1)], z_send)

    @pl.loop(0, n1 + n2)
    def _(k):
        drain(serve.at[k, pl.ds(1, ncol - 1)], ans_send.at[k])
        for way in range(2):
            for s in range(1, half + 1):
                drain(ring_block(k, s, way, s == half), ring_send.at[k, way, s - 1])


def lists_all(asked, ncol):
    return asked.at[pl.ds(1, ncol - 1)]


def body(
    features,
    neighbours,
    neighbour_mask,
    layer2_position,
    self_weight1,
    neigh_weight1,
    self_weight2,
    neigh_weight2,
):
    rows, width = features.shape
    hidden = self_weight1.shape[1]
    ny = lax.axis_size("grp")
    ncol = NX * ny * NC
    block = CAP * NZ
    slots = ncol * block
    chunk = CHUNK
    n1, n2 = width // chunk, hidden // chunk
    half = NZ // 2
    degree = neighbours.shape[1]
    window = 8 * block // LANES
    rank2 = rows // (NX * NZ)
    vmem = pltpu.VMEM
    dma = pltpu.SemaphoreType.DMA
    return pl.pallas_call(
        kernel,
        out_shape=jax.ShapeDtypeStruct((rows, hidden), BF),
        in_specs=[pl.BlockSpec(memory_space=vmem)] * 3
        + [pl.BlockSpec(memory_space=pl.ANY)] * 5,
        out_specs=pl.BlockSpec(memory_space=vmem),
        scratch_shapes=[
            vmem(self_weight1.shape, BF),
            vmem(neigh_weight1.shape, BF),
            vmem(self_weight2.shape, BF),
            vmem(neigh_weight2.shape, BF),
            vmem((n1 + n2, NZ * rows, chunk), BF),
            vmem((n1 + n2, ncol, block, chunk), BF),
            vmem((n1 + n2, ncol, block, chunk), BF),
            vmem((slots, NZ * rows), BF),
            vmem((rows, slots), jnp.int32),
            vmem((rows, slots), BF),
            vmem((rows, slots), BF),
            vmem((rows, LANES), F32),
            vmem((rows, LANES), F32),
            vmem((rows, LANES), F32),
            vmem((rows, LANES), F32),
            vmem((rows, degree), jnp.int32),
            vmem((rows, degree), jnp.int32),
            vmem((rows, degree), jnp.int32),
            vmem((slots // LANES, 1, LANES), jnp.int32),
            vmem((ncol, window, 1, LANES), jnp.int32),
            vmem((rows, hidden), F32),
            vmem((rows, hidden), BF),
            vmem((NX, NZ * rank2, hidden + LANES), BF),
            vmem((NX, NZ * rank2, hidden + LANES), BF),
            vmem((NZ, NX * rank2, hidden + LANES), BF),
            vmem((NZ, NX * rank2, hidden + LANES), BF),
            dma((n1 + 4,)),
            dma((n1 + n2, 2, half)),
            dma((n1 + n2, 2, half)),
            dma,
            dma,
            dma((n1 + n2,)),
            dma((n1 + n2,)),
            dma,
            dma,
            dma,
            dma,
        ],
        compiler_params=pltpu.CompilerParams(
            collective_id=0, has_side_effects=True, vmem_limit_bytes=56 * 2**20
        ),
    )(
        neighbours,
        neighbour_mask,
        layer2_position.reshape(1, rows),
        features,
        self_weight1,
        neigh_weight1,
        self_weight2,
        neigh_weight2,
    )


def solution(mesh):
    spread = P(("grp", "dev"), None)
    return jax.shard_map(
        body,
        mesh=mesh,
        in_specs=(spread, spread, spread, P(("grp", "dev")), P(), P(), P(), P()),
        out_specs=spread,
        check_vma=False,
    )
```

```python
import jax
import jax.numpy as jnp
from jax import lax
from jax.experimental import pallas as pl
from jax.experimental.pallas import tpu as pltpu
from jax.sharding import PartitionSpec as P

NX, NZ, NC = 4, 8, 2
CAP = 6
LANES = 128
BF = jnp.bfloat16
F32 = jnp.float32
MESH = pl.DeviceIdType.MESH


def iota(shape, dim):
    return lax.broadcasted_iota(jnp.int32, shape, dim)


def mm(a, b):
    return jnp.dot(a, b, preferred_element_type=F32)


def one_zero(cond):
    return jnp.where(cond, 1.0, 0.0).astype(BF)


def spans(first, units):
    cuts = [(first, 1)]
    at = first + 1
    while at < first + units:
        wide = 2 if at + 2 < first + units else 1
        cuts.append((at, wide))
        at += wide
    return cuts


def kernel(
    nb_ref,
    mk_ref,
    pos_ref,
    feat_hbm,
    ws1_hbm,
    wn1_hbm,
    ws2_hbm,
    wn2_hbm,
    out_ref,
    ws1,
    wn1,
    ws2,
    wn2,
    table,
    serve,
    ans,
    pick,
    key_ref,
    adj,
    adj2,
    loc,
    loc2,
    cnt2,
    slots,
    slot_p,
    slot_id,
    slot_row,
    lists,
    asked,
    acc,
    hid,
    pos_out,
    pos_in,
    fold,
    leave,
    land,
    load_sem,
    near_send,
    near_recv,
    ring_send,
    ring_recv,
    req_send,
    req_recv,
    pos_send,
    pos_recv,
    ans_send,
    ans_recv,
    out_send,
    out_recv,
):
    degree, rows = nb_ref.shape
    ny = lax.axis_size("grp")
    n_dev = NX * NZ * NC
    plane = ny * NC
    ncol = NX * plane
    block = CAP * NZ
    n1 = feat_hbm.shape[1] // LANES
    hidden_width = wn2.shape[0]
    n2 = hidden_width // LANES
    half = NZ // 2
    rank2 = rows // (NX * NZ)
    pieces1 = spans(0, n1)
    pieces2 = spans(n1, n2)
    me_y = lax.axis_index("grp")
    me_dev = lax.axis_index("dev")
    me_x = lax.div(me_dev, NZ * NC)
    me_z = lax.rem(lax.div(me_dev, NC), NZ)
    me_c = lax.rem(me_dev, NC)
    at_x = [lax.rem(me_x + k, NX) * (NZ * NC) for k in range(NX)]
    at_y = [lax.rem(me_y + k, ny) for k in range(ny)]
    at_z = [lax.rem(me_z + k, NZ) * NC for k in range(NZ)]
    at_c = [lax.rem(me_c + k, NC) for k in range(NC)]

    def ahead(d):
        return (
            at_y[d // NC % ny],
            at_x[d // plane] + at_z[0] + at_c[d % NC],
        )

    def behind(d):
        return (
            at_y[-(d // NC % ny) % ny],
            at_x[-(d // plane) % NX] + at_z[0] + at_c[-(d % NC) % NC],
        )

    def owner_at(d):
        return (me_y, at_x[d // NZ] + at_z[d % NZ] + me_c)

    def along_z(dz):
        return (me_y, at_x[0] + at_z[dz] + me_c)

    def drain(ref, sem):
        pltpu.make_async_copy(ref, ref, sem).wait()

    def send(src, dst, out, into, device):
        return pltpu.make_async_remote_copy(
            src_ref=src,
            dst_ref=dst,
            send_sem=out,
            recv_sem=into,
            device_id=device,
            device_id_type=MESH,
        )

    own = pl.ds(pl.multiple_of(me_z * rows, rows), rows)

    loads = []
    for u in range(n1):
        loads.append(
            pltpu.make_async_copy(
                feat_hbm.at[:, pl.ds(u * LANES, LANES)],
                table.at[u, own],
                load_sem.at[u],
            )
        )
    for k, (far, near) in enumerate(
        ((ws1_hbm, ws1), (wn1_hbm, wn1), (ws2_hbm, ws2), (wn2_hbm, wn2))
    ):
        loads.append(pltpu.make_async_copy(far, near, load_sem.at[n1 + k]))
    for u in range(n1):
        loads[u].start()

    barrier = pltpu.get_barrier_semaphore()
    peers = [along_z(dz) for dz in range(1, NZ)]
    peers += [ahead(d) for d in range(1, ncol)]
    peers += [owner_at(d) for d in range(1, NX * NZ) if d // NZ and d % NZ]
    for peer in peers:
        pl.semaphore_signal(barrier, inc=1, device_id=peer, device_id_type=MESH)
    for load in loads[n1:]:
        load.start()

    nb = nb_ref[...]
    mk = mk_ref[...]
    owner = nb // rows
    row = nb % rows
    o_y = owner // n_dev
    o_dev = owner % n_dev
    o_x = o_dev // (NZ * NC)
    o_z = o_dev // NC % NZ
    o_c = o_dev % NC
    mine = owner == me_y * n_dev + me_dev
    valid = mk > 0
    remote = valid & jnp.logical_not(mine)
    col = (
        ((me_x + NX - o_x) % NX) * plane
        + ((me_y + ny - o_y) % ny) * NC
        + (me_c + NC - o_c) % NC
    )
    far_col = jnp.where(remote, col, -4096)

    pack = LANES // ncol
    lane = iota((rows, LANES), 1)
    sub = iota((rows, LANES), 0)
    sooner = one_zero(sub < lane)
    ones = jnp.ones((rows, LANES), BF)
    same = lane % ncol == sub % ncol
    every = one_zero(same)
    before = one_zero(same & (lane // ncol < sub // ncol))
    so_far = jnp.zeros((rows, LANES), F32)
    slots[...] = jnp.full_like(slots, -1)
    for j in range(0, degree, pack):
        members = range(j, min(j + pack, degree))
        hot = jnp.zeros((rows, LANES), jnp.bool_)
        for s in members:
            hot = hot | (far_col[s : s + 1, :] == sub - (s - j) * ncol)
        hot = one_zero(hot)
        totals = mm(hot, ones)
        rank = (
            mm(hot, sooner)
            + mm(before, totals.astype(BF))
            + mm(every, so_far.astype(BF))
        )
        so_far = so_far + totals
        rank = rank * hot.astype(F32)
        for s in members:
            part = rank[(s - j) * ncol : (s - j + 1) * ncol, :]
            slots[0, s : s + 1, :] = jnp.sum(part, axis=0, keepdims=True).astype(jnp.int32)
    slots[0, 0:degree, :] = jnp.where(remote, col * block + slots[0, 0:degree, :], -1)
    slots[1, 0:degree, :] = o_z * rows + row + 1
    slots[2, 0:degree, :] = jnp.where(valid & mine, row, -1)
    slot_p[...] = slots[0].T
    slot_id[...] = slots[1].T
    slot_row[...] = slots[2].T
    count = jnp.sum(mk.astype(F32), axis=0, keepdims=True)
    diagonal = jnp.where(sub == lane, count, 0.0).astype(BF)
    cnt = mm(diagonal, ones)

    for u in range(n1):
        loads[u].wait()
    pl.semaphore_wait(barrier, len(peers))

    def wide_at(piece, z, start, size):
        first, wide = piece
        return table.at[
            pl.ds(first, wide), pl.ds(pl.multiple_of(z * rows + start, rows // 2), size)
        ]

    def near_all(layer, piece):
        mine_at = wide_at(piece, me_z, 0, rows)
        for dz in (4, 3, 5, 2, 6, 1, 7):
            send(
                mine_at, mine_at, near_send.at[layer], near_recv.at[layer], along_z(dz)
            ).start()

    def near_wait(layer, piece, sem):
        first, wide = piece
        drain(table.at[pl.ds(first, wide), pl.ds(0, (NZ - 1) * rows)], sem.at[layer])

    def ring_block(piece, s, way, last):
        back = -(s - 1) % NZ if way == 0 else (s - 1) % NZ
        z = lax.rem(me_z + back, NZ)
        if last:
            return wide_at(piece, z, way * (rows // 2), rows // 2)
        return wide_at(piece, z, 0, rows)

    def ring_op(piece, s):
        for way in range(2):
            if s > 1:
                drain(
                    ring_block(piece, s, way, False), ring_recv.at[piece[0], way, s - 2]
                )
            if s <= half:
                ref = ring_block(piece, s, way, s == half)
                send(
                    ref,
                    ref,
                    ring_send.at[piece[0], way, s - 1],
                    ring_recv.at[piece[0], way, s - 1],
                    along_z(1 if way == 0 else NZ - 1),
                ).start()

    def ring_end(piece):
        for way in range(2):
            drain(
                ring_block(piece, half + 1, way, True),
                ring_recv.at[piece[0], way, half - 1],
            )

    def turn(pieces, t):
        for p in range(1, len(pieces)):
            if 1 <= t - (p - 1) <= half:
                ring_op(pieces[p], t - (p - 1))

    near_all(0, pieces1[0])
    turn(pieces1, 1)

    tiles = ncol * block // LANES
    lists[...] = jnp.zeros_like(lists)

    @pl.loop(0, rows // 8)
    def _(i):
        at_rows = pl.ds(pl.multiple_of(i * 8, 8), 8)
        p8 = slot_p[at_rows, :]
        id8 = slot_id[at_rows, :]
        row8 = slot_row[at_rows, :]
        lane8 = iota((8, LANES), 1)
        p_all = [jnp.broadcast_to(p8[:, s : s + 1], (8, LANES)) for s in range(degree)]
        id_all = [jnp.broadcast_to(id8[:, s : s + 1], (8, LANES)) for s in range(degree)]
        for t in range(tiles):
            got = jnp.zeros((8, LANES), jnp.int32)
            for s in range(degree):
                got = jnp.where(p_all[s] == lane8 + t * LANES, id_all[s], got)
            key_ref[at_rows, t * LANES : (t + 1) * LANES] = got
            lists[t] = lists[t] + jnp.sum(got, axis=0, keepdims=True)
        near = jnp.zeros((8, LANES), F32)
        for s in range(degree):
            near = near + jnp.where(row8[:, s : s + 1] == lane8, 1.0, 0.0)
        loc[at_rows, :] = near

    window = 8 * block // LANES
    for d in range(1, ncol):
        send(
            lists.at[pl.ds(d // 8 * window, window)],
            asked.at[d],
            req_send,
            req_recv,
            behind(d),
        ).start()
    asked[0] = lists[0:window]
    turn(pieces1, 2)

    pos = pos_ref[...]
    t_dev = pos // rows % n_dev
    t_x = t_dev // (NZ * NC)
    t_z = t_dev // NC % NZ
    target = ((t_x + NX - me_x) % NX) * NZ + (t_z + NZ - me_z) % NZ
    hot_t = iota((NX * NZ, rows), 0) == target
    ahead_of = mm(one_zero(hot_t), sooner)
    rank_t = jnp.sum(jnp.where(hot_t, ahead_of, 0.0), axis=0, keepdims=True)
    move = one_zero(target * rank2 + rank_t.astype(jnp.int32) == sub)
    pos_8 = jnp.broadcast_to((pos % rows).astype(F32), (16, rows)).astype(BF)
    pos_t = lax.dot_general(
        pos_8, move, (((1,), (1,)), ((), ())), preferred_element_type=F32
    )
    pos_out[...] = pos_t[0:8, :]
    for d in range(1, NX * NZ):
        send(pos_out, pos_in.at[d], pos_send, pos_recv, owner_at(d)).start()
    pos_in[0] = pos_out[...]
    adj[...] = one_zero(key_ref[...] > 0)
    adj2[...] = mm(move, adj[...]).astype(BF)
    loc2[...] = mm(move, loc[...].astype(BF))
    cnt2[...] = mm(move, cnt.astype(BF))

    drain(asked.at[pl.ds(1, ncol - 1)], req_recv)
    turn(pieces1, 3)

    @pl.loop(0, ncol)
    def _(d):
        got = asked[d]
        spot = iota((block, LANES), 0) + lax.rem(d, 8) * block
        found = jnp.zeros((block, LANES), jnp.int32)
        for t in range(window):
            piece = jnp.broadcast_to(got[t], (block, LANES))
            found = found + jnp.where(iota((block, LANES), 1) + t * LANES == spot, piece, 0)
        found = jnp.sum(found, axis=1, keepdims=True)
        hit = iota((block, NZ * rows), 1) + 1 == found
        pick[pl.ds(pl.multiple_of(d * block, block), block), :] = one_zero(hit)

    def joined(ref, piece, *index):
        first, wide = piece
        return jnp.concatenate([ref[(u, *index)] for u in range(first, first + wide)], 1)

    def serve_piece(piece):
        first, wide = piece

        @pl.loop(0, NX)
        def _(j):
            some = pl.ds(pl.multiple_of(j * plane * block, plane * block), plane * block)
            picked = mm(pick[some, :], joined(table, piece)).astype(BF)
            picked = picked.reshape(plane, block, wide * LANES)
            for k in range(wide):
                serve[first + k, pl.ds(j * plane, plane)] = picked[
                    :, :, k * LANES : (k + 1) * LANES
                ]
            base = lax.rem(me_x + j, NX) * (NZ * NC) + at_z[0]
            for i in range(plane):
                cp = send(
                    serve.at[pl.ds(first, wide), j * plane + i],
                    ans.at[pl.ds(first, wide), j * plane + i],
                    ans_send.at[first],
                    ans_recv.at[first],
                    (at_y[i // NC], base + at_c[i % NC]),
                )
                if i == 0:
                    pl.when(j > 0)(cp.start)
                else:
                    cp.start()

        for k in range(wide):
            ans[first + k, 0] = serve[first + k, 0]

    def serve_layer(layer, pieces):
        near_wait(layer, pieces[0], near_recv)
        serve_piece(pieces[0])
        turn(pieces, half)
        for p in range(1, len(pieces)):
            ring_end(pieces[p])
            serve_piece(pieces[p])
            turn(pieces, half + p)

    def answers(piece, ref):
        return ref.at[pl.ds(piece[0], piece[1]), pl.ds(1, ncol - 1)]

    def mean(piece, adjacency, near, degrees):
        first, wide = piece
        drain(answers(piece, ans), ans_recv.at[first])
        rows_in = jnp.concatenate(
            [ans[first + k].reshape(ncol * block, LANES) for k in range(wide)], 1
        )
        summed = mm(adjacency[...], rows_in) + mm(near, joined(table, piece, own))
        return (summed / degrees).astype(BF)

    def cut(piece, start=0):
        return slice((piece[0] - start) * LANES, (piece[0] - start + piece[1]) * LANES)

    serve_layer(0, pieces1)
    loads[n1].wait()
    loads[n1 + 1].wait()
    x = jnp.concatenate([table[u, own, :] for u in range(n1)], 1)
    for q in pieces2:
        acc[:, cut(q, n1)] = mm(x, ws1[:, cut(q, n1)])
    near1 = loc[...].astype(BF)
    degrees1 = cnt[:, 0:1]
    for q in pieces1[:-1]:
        acc[...] += mm(mean(q, adj, near1, degrees1), wn1[cut(q), :])
    m = mean(pieces1[-1], adj, near1, degrees1)
    for i, q in enumerate(pieces2):
        total = acc[:, cut(q, n1)] + mm(m, wn1[cut(pieces1[-1]), cut(q, n1)])
        total = jnp.maximum(total, 0.0).astype(BF)
        for k in range(q[1]):
            table[q[0] + k, own, :] = total[:, k * LANES : (k + 1) * LANES]
        if i == 0:
            near_all(1, q)
        if i == 1:
            turn(pieces2, 1)
    turn(pieces2, 2)
    hid[...] = mm(
        move, jnp.concatenate([table[n1 + u, own, :] for u in range(n2)], 1)
    ).astype(BF)
    turn(pieces2, 3)
    serve_layer(1, pieces2)
    loads[n1 + 2].wait()
    loads[n1 + 3].wait()
    for q in pieces2:
        acc[:, cut(q, n1)] = mm(hid[...], ws2[:, cut(q, n1)])
    drain(pos_in.at[pl.ds(1, NX * NZ - 1)], pos_recv)
    near2 = loc2[...].astype(BF)
    for q in pieces2:
        acc[...] += mm(mean(q, adj2, near2, cnt2[:, 0:1]), wn2[cut(q, n1), :])

    fold_rows = 2 * rank2
    pairs = NX * NZ // 2
    low = sub % fold_rows < rank2
    for t in range(n2 // 2):
        a = acc[:, 2 * t * LANES : (2 * t + 1) * LANES]
        b = acc[:, (2 * t + 1) * LANES : (2 * t + 2) * LANES]
        inner = slice(t * fold_rows, (t + 1) * fold_rows)
        first = jnp.where(low, a, pltpu.roll(b, rank2, 0))
        second = jnp.where(low, pltpu.roll(a, rows - rank2, 0), b)
        fold[0:pairs, inner, :] = first.reshape(pairs, fold_rows, LANES)
        fold[pairs:, inner, :] = second.reshape(pairs, fold_rows, LANES)
    leave[...] = fold[...].astype(BF)
    for d in range(1, NX * NZ):
        send(
            leave.at[d % 2 * pairs + d // 2],
            land.at[d % 2 * pairs + d // 2],
            out_send,
            out_recv,
            owner_at(d),
        ).start()
    land[0] = leave[0]

    here = jnp.zeros((1, LANES), F32)
    for d in range(NX * NZ):
        mine_d = iota((1, LANES), 1) // rank2 == d
        here = jnp.where(mine_d, pos_in[d, 0:1, :], here)
    put = one_zero(here == sub.astype(F32))

    drain(land.at[pl.ds(1, 2 * pairs - 1)], out_recv)
    fold[...] = land[...].astype(F32)
    for t in range(n2 // 2):
        inner = slice(t * fold_rows, (t + 1) * fold_rows)
        first = fold[0:pairs, inner, :].reshape(rows, LANES)
        second = fold[pairs:, inner, :].reshape(rows, LANES)
        a = jnp.where(low, first, pltpu.roll(second, rank2, 0))
        b = jnp.where(low, pltpu.roll(first, rows - rank2, 0), second)
        both = jnp.concatenate([a, b], 1).astype(BF)
        out_ref[:, 2 * t * LANES : (2 * t + 2) * LANES] = mm(put, both).astype(BF)

    drain(asked.at[pl.ds(1, ncol - 1)], req_send)
    drain(pos_in.at[pl.ds(1, NX * NZ - 1)], pos_send)
    drain(leave.at[pl.ds(1, 2 * pairs - 1)], out_send)
    for layer, pieces in enumerate((pieces1, pieces2)):
        near_wait(layer, pieces[0], near_send)
        for q in pieces:
            drain(answers(q, serve), ans_send.at[q[0]])
        for q in pieces[1:]:
            for way in range(2):
                for s in range(1, half + 1):
                    drain(
                        ring_block(q, s, way, s == half), ring_send.at[q[0], way, s - 1]
                    )


def body(
    features,
    neighbours,
    neighbour_mask,
    layer2_position,
    self_weight1,
    neigh_weight1,
    self_weight2,
    neigh_weight2,
):
    rows, width = features.shape
    hidden = self_weight1.shape[1]
    ny = lax.axis_size("grp")
    ncol = NX * ny * NC
    block = CAP * NZ
    slots = ncol * block
    units = (width + hidden) // LANES
    half = NZ // 2
    window = 8 * block // LANES
    rank2 = rows // (NX * NZ)
    deep = hidden // LANES * rank2
    vmem = pltpu.VMEM
    dma = pltpu.SemaphoreType.DMA
    return pl.pallas_call(
        kernel,
        out_shape=jax.ShapeDtypeStruct((rows, hidden), BF),
        in_specs=[pl.BlockSpec(memory_space=vmem)] * 3
        + [pl.BlockSpec(memory_space=pl.ANY)] * 5,
        out_specs=pl.BlockSpec(memory_space=vmem),
        scratch_shapes=[
            vmem(self_weight1.shape, BF),
            vmem(neigh_weight1.shape, BF),
            vmem(self_weight2.shape, BF),
            vmem(neigh_weight2.shape, BF),
            vmem((units, NZ * rows, LANES), BF),
            vmem((units, ncol, block, LANES), BF),
            vmem((units, ncol, block, LANES), BF),
            vmem((slots, NZ * rows), BF),
            vmem((rows, slots), jnp.int32),
            vmem((rows, slots), BF),
            vmem((rows, slots), BF),
            vmem((rows, LANES), F32),
            vmem((rows, LANES), F32),
            vmem((rows, LANES), F32),
            vmem((3, 32, rows), jnp.int32),
            vmem((rows, 32), jnp.int32),
            vmem((rows, 32), jnp.int32),
            vmem((rows, 32), jnp.int32),
            vmem((slots // LANES, 1, LANES), jnp.int32),
            vmem((ncol, window, 1, LANES), jnp.int32),
            vmem((rows, hidden), F32),
            vmem((rows, hidden), BF),
            vmem((8, LANES), F32),
            vmem((NX * NZ, 8, LANES), F32),
            vmem((NX * NZ, deep, LANES), F32),
            vmem((NX * NZ, deep, LANES), BF),
            vmem((NX * NZ, deep, LANES), BF),
            dma((width // LANES + 4,)),
            dma((2,)),
            dma((2,)),
            dma((units, 2, half)),
            dma((units, 2, half)),
            dma,
            dma,
            dma,
            dma,
            dma((units,)),
            dma((units,)),
            dma,
            dma,
        ],
        compiler_params=pltpu.CompilerParams(
            collective_id=0, has_side_effects=True, vmem_limit_bytes=56 * 2**20
        ),
    )(
        neighbours.T,
        neighbour_mask.T,
        layer2_position.reshape(1, rows),
        features,
        self_weight1,
        neigh_weight1,
        self_weight2,
        neigh_weight2,
    )


def solution(mesh):
    spread = P(("grp", "dev"), None)
    return jax.shard_map(
        body,
        mesh=mesh,
        in_specs=(spread, spread, spread, P(("grp", "dev")), P(), P(), P(), P()),
        out_specs=spread,
        check_vma=False,
    )
```

```python
import jax
import jax.numpy as jnp
from jax import lax
from jax.experimental import pallas as pl
from jax.experimental.pallas import tpu as pltpu
from jax.sharding import PartitionSpec as P

NX, NZ, NC = 4, 8, 2
CAP = 6
LANES = 128
BF = jnp.bfloat16
F32 = jnp.float32
MESH = pl.DeviceIdType.MESH


def iota(shape, dim):
    return lax.broadcasted_iota(jnp.int32, shape, dim)


def mm(a, b):
    return jnp.dot(a, b, preferred_element_type=F32)


def one_zero(cond):
    return jnp.where(cond, 1.0, 0.0).astype(BF)


PLACES = (1, NZ - 1, 0, 2, NZ - 2, 3, NZ - 3, 4)
OWN = PLACES.index(0)
ROW = 16


def place_of(dz):
    return PLACES.index(dz % NZ)


def kernel(
    nb_ref,
    mk_ref,
    pos_ref,
    feat_hbm,
    ws1_hbm,
    wn1_hbm,
    ws2_hbm,
    wn2_hbm,
    out_ref,
    ws1,
    wn1,
    ws2,
    wn2,
    table1,
    table2,
    serve1,
    serve2,
    ans1,
    ans2,
    pick,
    key_ref,
    adj,
    adj2,
    loc,
    loc2,
    cnt2,
    slots,
    slot_p,
    slot_id,
    slot_row,
    lists,
    asked,
    acc,
    hid,
    pos_out,
    pos_in,
    fold,
    leave,
    land,
    load_sem,
    ring_send,
    ring_recv,
    req_send,
    req_recv,
    pos_send,
    pos_recv,
    ans_send,
    ans_recv,
    out_send,
    out_recv,
):
    degree, rows = nb_ref.shape
    ny = lax.axis_size("grp")
    n_dev = NX * NZ * NC
    plane = ny * NC
    ncol = NX * plane
    block = CAP * NZ
    blocks = block // ROW
    per_block = ncol * ROW
    hidden_width = wn2.shape[0]
    n2 = hidden_width // LANES
    half = NZ // 2
    rank2 = rows // (NX * NZ)
    me_y = lax.axis_index("grp")
    me_dev = lax.axis_index("dev")
    me_x = lax.div(me_dev, NZ * NC)
    me_z = lax.rem(lax.div(me_dev, NC), NZ)
    me_c = lax.rem(me_dev, NC)
    at_x = [lax.rem(me_x + k, NX) * (NZ * NC) for k in range(NX)]
    at_y = [lax.rem(me_y + k, ny) for k in range(ny)]
    at_z = [lax.rem(me_z + k, NZ) * NC for k in range(NZ)]
    at_c = [lax.rem(me_c + k, NC) for k in range(NC)]

    def ahead(d):
        return (
            at_y[d // NC % ny],
            at_x[d // plane] + at_z[0] + at_c[d % NC],
        )

    def behind(d):
        return (
            at_y[-(d // NC % ny) % ny],
            at_x[-(d // plane) % NX] + at_z[0] + at_c[-(d % NC) % NC],
        )

    def owner_at(d):
        return (me_y, at_x[d // NZ] + at_z[d % NZ] + me_c)

    def along_z(dz):
        return (me_y, at_x[0] + at_z[dz] + me_c)

    def drain(ref, sem):
        pltpu.make_async_copy(ref, ref, sem).wait()

    def send(src, dst, out, into, device):
        return pltpu.make_async_remote_copy(
            src_ref=src,
            dst_ref=dst,
            send_sem=out,
            recv_sem=into,
            device_id=device,
            device_id_type=MESH,
        )

    own = slice(OWN * rows, (OWN + 1) * rows)

    loads = [
        pltpu.make_async_copy(far, near, load_sem.at[k])
        for k, (far, near) in enumerate(
            (
                (feat_hbm, table1.at[pl.ds(OWN * rows, rows)]),
                (ws1_hbm, ws1),
                (wn1_hbm, wn1),
                (ws2_hbm, ws2),
                (wn2_hbm, wn2),
            )
        )
    ]
    loads[0].start()

    barrier = pltpu.get_barrier_semaphore()
    peers = [along_z(dz) for dz in range(1, NZ)]
    peers += [ahead(d) for d in range(1, ncol)]
    peers += [owner_at(d) for d in range(1, NX * NZ) if d // NZ and d % NZ]
    for peer in peers:
        pl.semaphore_signal(barrier, inc=1, device_id=peer, device_id_type=MESH)
    for load in loads[1:]:
        load.start()

    nb = nb_ref[...]
    mk = mk_ref[...]
    owner = nb // rows
    row = nb % rows
    o_y = owner // n_dev
    o_dev = owner % n_dev
    o_x = o_dev // (NZ * NC)
    o_z = o_dev // NC % NZ
    o_c = o_dev % NC
    mine = owner == me_y * n_dev + me_dev
    valid = mk > 0
    remote = valid & jnp.logical_not(mine)
    col = (
        ((me_x + NX - o_x) % NX) * plane
        + ((me_y + ny - o_y) % ny) * NC
        + (me_c + NC - o_c) % NC
    )
    away = (o_z + NZ - me_z) % NZ
    nearness = jnp.zeros_like(away)
    for k, dz in enumerate(PLACES):
        nearness = jnp.where(away == dz, k, nearness)

    lane = iota((rows, LANES), 1)
    sub = iota((rows, LANES), 0)
    sooner = one_zero(sub < lane)
    ones = jnp.ones((rows, LANES), BF)
    sooner_all = jnp.concatenate([sooner, ones], 1)
    slots[...] = jnp.full_like(slots, -1)
    slots[3, 0:degree, :] = jnp.where(remote, nearness * ncol + col, -1)

    def rank_slot(s, so_far):
        hot = slots[3, pl.ds(s, 1), :] == iota((NZ * ncol, rows), 0)
        counted = mm(one_zero(hot), sooner_all)
        rank = jnp.where(hot, counted[:, :rows] + so_far, 0.0)
        slots[0, pl.ds(s, 1), :] = jnp.sum(rank, axis=0, keepdims=True).astype(jnp.int32)
        return so_far + counted[:, rows:]

    lax.fori_loop(0, degree, rank_slot, jnp.zeros((NZ * ncol, rows), F32))
    spot = nearness * CAP + slots[0, 0:degree, :]
    slots[0, 0:degree, :] = jnp.where(
        remote, spot // ROW * per_block + col * ROW + spot % ROW, -1
    )
    slots[1, 0:degree, :] = nearness * rows + row + 1
    slots[2, 0:degree, :] = jnp.where(valid & mine, row, -1)
    slot_p[...] = slots[0].T
    slot_id[...] = slots[1].T
    slot_row[...] = slots[2].T
    count = jnp.sum(mk.astype(F32), axis=0, keepdims=True)
    diagonal = jnp.where(sub == lane, count, 0.0).astype(BF)
    cnt = mm(diagonal, ones)

    loads[0].wait()
    pl.semaphore_wait(barrier, len(peers))

    def part_of(table, dz, h):
        wide = table.shape[1] // 2
        return table.at[pl.ds(place_of(dz) * rows, rows), pl.ds(h * wide, wide)]

    def moves(s):
        for way, sign in enumerate((-1, 1)):
            for h in range(2):
                if s < half or h == way:
                    yield way, sign, h

    def ring_start(layer, table, s, halves=(0, 1)):
        for way, sign, h in moves(s):
            if h in halves:
                send(
                    part_of(table, sign * (s - 1), h),
                    part_of(table, sign * s, h),
                    ring_send.at[layer, way, s - 1, h],
                    ring_recv.at[layer, way, s - 1, h],
                    along_z(1 if way == 0 else NZ - 1),
                ).start()

    def ring_wait(layer, table, s, halves=(0, 1)):
        for way, sign, h in moves(s):
            if h in halves:
                drain(part_of(table, sign * s, h), ring_recv.at[layer, way, s - 1, h])

    def ring_left(layer, table):
        for s in range(1, half + 1):
            for way, sign, h in moves(s):
                drain(
                    part_of(table, sign * (s - 1), h), ring_send.at[layer, way, s - 1, h]
                )

    ring_start(0, table1, 1)

    tiles = ncol * block // LANES
    lists[...] = jnp.zeros_like(lists)

    @pl.loop(0, rows // 8)
    def _(i):
        at_rows = pl.ds(pl.multiple_of(i * 8, 8), 8)
        p8 = slot_p[at_rows, :]
        id8 = slot_id[at_rows, :]
        row8 = slot_row[at_rows, :]
        lane8 = iota((8, LANES), 1)
        p_all = [jnp.broadcast_to(p8[:, s : s + 1], (8, LANES)) for s in range(degree)]
        id_all = [jnp.broadcast_to(id8[:, s : s + 1], (8, LANES)) for s in range(degree)]
        for t in range(tiles):
            got = jnp.zeros((8, LANES), jnp.int32)
            for s in range(degree):
                got = jnp.where(p_all[s] == lane8 + t * LANES, id_all[s], got)
            key_ref[at_rows, t * LANES : (t + 1) * LANES] = got
            at_list = t % (tiles // blocks) * blocks + t // (tiles // blocks)
            lists[at_list] = lists[at_list] + jnp.sum(got, axis=0, keepdims=True)
        near = jnp.zeros((8, LANES), F32)
        for s in range(degree):
            near = near + jnp.where(row8[:, s : s + 1] == lane8, 1.0, 0.0)
        loc[at_rows, :] = near

    window = blocks
    for d in range(1, ncol):
        send(
            lists.at[pl.ds(d // 8 * window, window)],
            asked.at[d],
            req_send,
            req_recv,
            behind(d),
        ).start()
    asked[0] = lists[0:window]
    ring_wait(0, table1, 1, (0,))
    ring_start(0, table1, 2, (0,))

    pos = pos_ref[...]
    t_dev = pos // rows % n_dev
    t_x = t_dev // (NZ * NC)
    t_z = t_dev // NC % NZ
    target = ((t_x + NX - me_x) % NX) * NZ + (t_z + NZ - me_z) % NZ
    hot_t = iota((NX * NZ, rows), 0) == target
    ahead_of = mm(one_zero(hot_t), sooner)
    rank_t = jnp.sum(jnp.where(hot_t, ahead_of, 0.0), axis=0, keepdims=True)
    move = one_zero(target * rank2 + rank_t.astype(jnp.int32) == sub)
    pos_8 = jnp.broadcast_to((pos % rows).astype(F32), (16, rows)).astype(BF)
    pos_t = lax.dot_general(
        pos_8, move, (((1,), (1,)), ((), ())), preferred_element_type=F32
    )
    pos_out[...] = pos_t[0:8, :]
    for d in range(1, NX * NZ):
        send(pos_out, pos_in.at[d], pos_send, pos_recv, owner_at(d)).start()
    pos_in[0] = pos_out[...]
    adj[...] = one_zero(key_ref[...] > 0)
    adj2[...] = mm(move, adj[...]).astype(BF)
    loc2[...] = mm(move, loc[...].astype(BF))
    cnt2[...] = mm(move, cnt.astype(BF))

    drain(asked.at[pl.ds(1, ncol - 1)], req_recv)

    reach = []
    for b in range(blocks):
        first, last = b * ROW // CAP, ((b + 1) * ROW - 1) // CAP
        reach.append((first * rows, (last + 1 - first) * rows))

    @pl.loop(0, ncol)
    def _(d):
        got = asked[d]
        spot = iota((ROW, LANES), 0) + lax.rem(d, 8) * ROW
        for b in range(blocks):
            first, deep = reach[b]
            piece = jnp.broadcast_to(got[b], (ROW, LANES))
            found = jnp.where(iota((ROW, LANES), 1) == spot, piece, 0)
            found = jnp.sum(found, axis=1, keepdims=True)
            hit = iota((ROW, deep), 1) + (first + 1) == found
            some = pl.ds(pl.multiple_of(d * ROW, ROW), ROW)
            pick[b, some, 0:deep] = one_zero(hit)

    def serve_block(layer, table, serve, b, halves):
        first, deep = reach[b]
        wide = table.shape[1] // 2
        at_col, n_col = halves[0] * wide, len(halves) * wide

        @pl.loop(0, NX)
        def _(j):
            some = pl.ds(pl.multiple_of(j * plane * ROW, plane * ROW), plane * ROW)
            picked = mm(
                pick[b, some, 0:deep],
                table[first : first + deep, at_col : at_col + n_col],
            ).astype(BF)
            serve[b, pl.ds(j * plane, plane), :, at_col : at_col + n_col] = picked.reshape(
                plane, ROW, n_col
            )
            base = lax.rem(me_x + j, NX) * (NZ * NC) + at_z[0]
            for i in range(plane):
                cp = send(
                    serve.at[b, j * plane + i, :, pl.ds(at_col, n_col)],
                    (ans1, ans2)[layer].at[b, j * plane + i, :, pl.ds(at_col, n_col)],
                    ans_send.at[layer, b, halves[0]],
                    ans_recv.at[layer, b, halves[0]],
                    (at_y[i // NC], base + at_c[i % NC]),
                )
                if i == 0:
                    pl.when(j > 0)(cp.start)
                else:
                    cp.start()

    def serve_layer(layer, table, serve, ans):
        serve_block(layer, table, serve, 0, (0,))
        ring_wait(layer, table, 1, (1,))
        ring_start(layer, table, 2, (1,))
        serve_block(layer, table, serve, 0, (1,))
        ring_wait(layer, table, 2)
        ring_start(layer, table, 3)
        ring_wait(layer, table, 3)
        ring_start(layer, table, 4)
        serve_block(layer, table, serve, 1, (0, 1))
        ring_wait(layer, table, 4)
        serve_block(layer, table, serve, 2, (0, 1))
        for b in range(blocks):
            ans[b, 0] = serve[b, 0]

    def answers(ref, b, halves):
        wide = ref.shape[3] // 2
        return ref.at[
            b, pl.ds(1, ncol - 1), :, pl.ds(halves[0] * wide, len(halves) * wide)
        ]

    parts = ((0, (0,)), (0, (1,)), (1, (0, 1)), (2, (0, 1)))

    def summed(layer, ans, b, adjacency):
        for part in parts:
            if part[0] == b:
                drain(answers(ans, *part), ans_recv.at[layer, b, part[1][0]])
        return mm(
            adjacency[:, b * per_block : (b + 1) * per_block],
            ans[b].reshape(per_block, ans.shape[3]),
        )

    serve_layer(0, table1, serve1, ans1)
    loads[1].wait()
    loads[2].wait()
    x = table1[own, :]
    acc[...] = mm(x, ws1[...])
    total = mm(loc[...].astype(BF), x)
    for b in range(blocks):
        total = total + summed(0, ans1, b, adj)
    m = (total / cnt[:, 0:1]).astype(BF)
    wide = hidden_width // 2
    for h in range(2):
        cols = slice(h * wide, (h + 1) * wide)
        total = acc[:, cols] + mm(m, wn1[:, cols])
        table2[own, cols] = jnp.maximum(total, 0.0).astype(BF)
        ring_start(1, table2, 1, (h,))
    hid[...] = mm(move, table2[own, :]).astype(BF)
    ring_wait(1, table2, 1, (0,))
    ring_start(1, table2, 2, (0,))
    serve_layer(1, table2, serve2, ans2)
    loads[3].wait()
    loads[4].wait()
    acc[...] = mm(hid[...], ws2[...])
    drain(pos_in.at[pl.ds(1, NX * NZ - 1)], pos_recv)
    total = mm(loc2[...].astype(BF), table2[own, :])
    for b in range(blocks):
        total = total + summed(1, ans2, b, adj2)
    m = (total / cnt2[:, 0:1]).astype(BF)
    acc[...] += mm(m, wn2[...])

    fold_rows = 2 * rank2
    pairs = NX * NZ // 2
    low = sub % fold_rows < rank2
    for t in range(n2 // 2):
        a = acc[:, 2 * t * LANES : (2 * t + 1) * LANES]
        b = acc[:, (2 * t + 1) * LANES : (2 * t + 2) * LANES]
        inner = slice(t * fold_rows, (t + 1) * fold_rows)
        first = jnp.where(low, a, pltpu.roll(b, rank2, 0))
        second = jnp.where(low, pltpu.roll(a, rows - rank2, 0), b)
        fold[0:pairs, inner, :] = first.reshape(pairs, fold_rows, LANES)
        fold[pairs:, inner, :] = second.reshape(pairs, fold_rows, LANES)
    leave[...] = fold[...].astype(BF)
    for d in range(1, NX * NZ):
        send(
            leave.at[d % 2 * pairs + d // 2],
            land.at[d % 2 * pairs + d // 2],
            out_send,
            out_recv,
            owner_at(d),
        ).start()
    land[0] = leave[0]

    here = jnp.zeros((1, LANES), F32)
    for d in range(NX * NZ):
        mine_d = iota((1, LANES), 1) // rank2 == d
        here = jnp.where(mine_d, pos_in[d, 0:1, :], here)
    put = one_zero(here == sub.astype(F32))

    drain(land.at[pl.ds(1, 2 * pairs - 1)], out_recv)
    fold[...] = land[...].astype(F32)
    for t in range(n2 // 2):
        inner = slice(t * fold_rows, (t + 1) * fold_rows)
        first = fold[0:pairs, inner, :].reshape(rows, LANES)
        second = fold[pairs:, inner, :].reshape(rows, LANES)
        a = jnp.where(low, first, pltpu.roll(second, rank2, 0))
        b = jnp.where(low, pltpu.roll(first, rows - rank2, 0), second)
        both = jnp.concatenate([a, b], 1).astype(BF)
        out_ref[:, 2 * t * LANES : (2 * t + 2) * LANES] = mm(put, both).astype(BF)

    drain(asked.at[pl.ds(1, ncol - 1)], req_send)
    drain(pos_in.at[pl.ds(1, NX * NZ - 1)], pos_send)
    drain(leave.at[pl.ds(1, 2 * pairs - 1)], out_send)
    for layer, table, serve in ((0, table1, serve1), (1, table2, serve2)):
        ring_left(layer, table)
        for part in parts:
            drain(answers(serve, *part), ans_send.at[layer, part[0], part[1][0]])


def body(
    features,
    neighbours,
    neighbour_mask,
    layer2_position,
    self_weight1,
    neigh_weight1,
    self_weight2,
    neigh_weight2,
):
    rows, width = features.shape
    hidden = self_weight1.shape[1]
    ny = lax.axis_size("grp")
    ncol = NX * ny * NC
    block = CAP * NZ
    slots = ncol * block
    blocks = block // ROW
    half = NZ // 2
    rank2 = rows // (NX * NZ)
    deep = hidden // LANES * rank2
    vmem = pltpu.VMEM
    dma = pltpu.SemaphoreType.DMA
    return pl.pallas_call(
        kernel,
        out_shape=jax.ShapeDtypeStruct((rows, hidden), BF),
        in_specs=[pl.BlockSpec(memory_space=vmem)] * 3
        + [pl.BlockSpec(memory_space=pl.ANY)] * 5,
        out_specs=pl.BlockSpec(memory_space=vmem),
        scratch_shapes=[
            vmem(self_weight1.shape, BF),
            vmem(neigh_weight1.shape, BF),
            vmem(self_weight2.shape, BF),
            vmem(neigh_weight2.shape, BF),
            vmem((NZ * rows, width), BF),
            vmem((NZ * rows, hidden), BF),
            vmem((blocks, ncol, ROW, width), BF),
            vmem((blocks, ncol, ROW, hidden), BF),
            vmem((blocks, ncol, ROW, width), BF),
            vmem((blocks, ncol, ROW, hidden), BF),
            vmem((blocks, ncol * ROW, 4 * rows), BF),
            vmem((rows, slots), jnp.int32),
            vmem((rows, slots), BF),
            vmem((rows, slots), BF),
            vmem((rows, LANES), F32),
            vmem((rows, LANES), F32),
            vmem((rows, LANES), F32),
            vmem((4, 32, rows), jnp.int32),
            vmem((rows, 32), jnp.int32),
            vmem((rows, 32), jnp.int32),
            vmem((rows, 32), jnp.int32),
            vmem((slots // LANES, 1, LANES), jnp.int32),
            vmem((ncol, blocks, 1, LANES), jnp.int32),
            vmem((rows, hidden), F32),
            vmem((rows, hidden), BF),
            vmem((8, LANES), F32),
            vmem((NX * NZ, 8, LANES), F32),
            vmem((NX * NZ, deep, LANES), F32),
            vmem((NX * NZ, deep, LANES), BF),
            vmem((NX * NZ, deep, LANES), BF),
            dma((5,)),
            dma((2, 2, half, 2)),
            dma((2, 2, half, 2)),
            dma,
            dma,
            dma,
            dma,
            dma((2, blocks, 2)),
            dma((2, blocks, 2)),
            dma,
            dma,
        ],
        compiler_params=pltpu.CompilerParams(
            collective_id=0, has_side_effects=True, vmem_limit_bytes=56 * 2**20
        ),
    )(
        neighbours.T,
        neighbour_mask.T,
        layer2_position.reshape(1, rows),
        features,
        self_weight1,
        neigh_weight1,
        self_weight2,
        neigh_weight2,
    )


def solution(mesh):
    spread = P(("grp", "dev"), None)
    return jax.shard_map(
        body,
        mesh=mesh,
        in_specs=(spread, spread, spread, P(("grp", "dev")), P(), P(), P(), P()),
        out_specs=spread,
        check_vma=False,
    )
```

```python
import jax
import jax.numpy as jnp
from jax import lax
from jax.experimental import pallas as pl
from jax.experimental.pallas import tpu as pltpu
from jax.sharding import PartitionSpec as P

NX, NZ, NC = 4, 8, 2
CAP = 6
LANES = 128
BF = jnp.bfloat16
F32 = jnp.float32
MESH = pl.DeviceIdType.MESH


def iota(shape, dim):
    return lax.broadcasted_iota(jnp.int32, shape, dim)


def mm(a, b):
    return jnp.dot(a, b, preferred_element_type=F32)


def one_zero(cond):
    return jnp.where(cond, 1.0, 0.0).astype(BF)


PLACES = (1, NZ - 1, 0, 2, NZ - 2, 3, NZ - 3, 4)
OWN = PLACES.index(0)
ROW = 16


def place_of(dz):
    return PLACES.index(dz % NZ)


def kernel(
    nb_ref,
    mk_ref,
    pos_ref,
    feat_hbm,
    ws1_hbm,
    wn1_hbm,
    ws2_hbm,
    wn2_hbm,
    out_ref,
    ws1,
    wn1,
    ws2,
    wn2,
    table1,
    table2,
    serve1,
    serve2,
    ans1,
    ans2,
    pick,
    key_ref,
    adj,
    adj2,
    loc,
    loc2,
    cnt2,
    slots,
    slot_p,
    slot_id,
    slot_row,
    lists,
    asked,
    acc,
    hid,
    pos_out,
    pos_in,
    fold,
    leave,
    land,
    load_sem,
    ring_send,
    ring_recv,
    req_send,
    req_recv,
    pos_send,
    pos_recv,
    ans_send,
    ans_recv,
    out_send,
    out_recv,
):
    degree, rows = nb_ref.shape
    ny = lax.axis_size("grp")
    n_dev = NX * NZ * NC
    plane = ny * NC
    ncol = NX * plane
    block = CAP * NZ
    blocks = block // ROW
    per_block = ncol * ROW
    hidden_width = wn2.shape[0]
    n2 = hidden_width // LANES
    half = NZ // 2
    rank2 = rows // (NX * NZ)
    me_y = lax.axis_index("grp")
    me_dev = lax.axis_index("dev")
    me_x = lax.div(me_dev, NZ * NC)
    me_z = lax.rem(lax.div(me_dev, NC), NZ)
    me_c = lax.rem(me_dev, NC)
    at_x = [lax.rem(me_x + k, NX) * (NZ * NC) for k in range(NX)]
    at_y = [lax.rem(me_y + k, ny) for k in range(ny)]
    at_z = [lax.rem(me_z + k, NZ) * NC for k in range(NZ)]
    at_c = [lax.rem(me_c + k, NC) for k in range(NC)]

    def ahead(d):
        return (
            at_y[d // NC % ny],
            at_x[d // plane] + at_z[0] + at_c[d % NC],
        )

    def behind(d):
        return (
            at_y[-(d // NC % ny) % ny],
            at_x[-(d // plane) % NX] + at_z[0] + at_c[-(d % NC) % NC],
        )

    def owner_at(d):
        return (me_y, at_x[d // NZ] + at_z[d % NZ] + me_c)

    def along_z(dz):
        return (me_y, at_x[0] + at_z[dz] + me_c)

    def drain(ref, sem):
        pltpu.make_async_copy(ref, ref, sem).wait()

    def send(src, dst, out, into, device):
        return pltpu.make_async_remote_copy(
            src_ref=src,
            dst_ref=dst,
            send_sem=out,
            recv_sem=into,
            device_id=device,
            device_id_type=MESH,
        )

    own = slice(OWN * rows, (OWN + 1) * rows)

    loads = [
        pltpu.make_async_copy(far, near, load_sem.at[k])
        for k, (far, near) in enumerate(
            (
                (feat_hbm, table1.at[pl.ds(OWN * rows, rows)]),
                (ws1_hbm, ws1),
                (wn1_hbm, wn1),
                (ws2_hbm, ws2),
                (wn2_hbm, wn2),
            )
        )
    ]
    loads[0].start()

    barrier = pltpu.get_barrier_semaphore()
    peers = [along_z(dz) for dz in range(1, NZ)]
    peers += [ahead(d) for d in range(1, ncol)]
    peers += [owner_at(d) for d in range(1, NX * NZ) if d // NZ and d % NZ]
    for peer in peers:
        pl.semaphore_signal(barrier, inc=1, device_id=peer, device_id_type=MESH)
    for load in loads[1:]:
        load.start()

    nb = nb_ref[...]
    mk = mk_ref[...]
    owner = nb // rows
    row = nb % rows
    o_y = owner // n_dev
    o_dev = owner % n_dev
    o_x = o_dev // (NZ * NC)
    o_z = o_dev // NC % NZ
    o_c = o_dev % NC
    mine = owner == me_y * n_dev + me_dev
    valid = mk > 0
    remote = valid & jnp.logical_not(mine)
    col = (
        ((me_x + NX - o_x) % NX) * plane
        + ((me_y + ny - o_y) % ny) * NC
        + (me_c + NC - o_c) % NC
    )
    away = (o_z + NZ - me_z) % NZ
    nearness = jnp.zeros_like(away)
    for k, dz in enumerate(PLACES):
        nearness = jnp.where(away == dz, k, nearness)

    lane = iota((rows, LANES), 1)
    sub = iota((rows, LANES), 0)
    sooner = one_zero(sub < lane)
    ones = jnp.ones((rows, LANES), BF)
    sooner_all = jnp.concatenate([sooner, ones], 1)
    slots[...] = jnp.full_like(slots, -1)
    slots[3, 0:degree, :] = jnp.where(remote, nearness * ncol + col, -1)

    def rank_slot(s, so_far):
        hot = slots[3, pl.ds(s, 1), :] == iota((NZ * ncol, rows), 0)
        counted = mm(one_zero(hot), sooner_all)
        rank = jnp.where(hot, counted[:, :rows] + so_far, 0.0)
        slots[0, pl.ds(s, 1), :] = jnp.sum(rank, axis=0, keepdims=True).astype(jnp.int32)
        return so_far + counted[:, rows:]

    lax.fori_loop(0, degree, rank_slot, jnp.zeros((NZ * ncol, rows), F32))
    spot = nearness * CAP + slots[0, 0:degree, :]
    slots[0, 0:degree, :] = jnp.where(
        remote, spot // ROW * per_block + col * ROW + spot % ROW, -1
    )
    slots[1, 0:degree, :] = nearness * rows + row + 1
    slots[2, 0:degree, :] = jnp.where(valid & mine, row, -1)
    slot_p[...] = slots[0].T
    slot_id[...] = slots[1].T
    slot_row[...] = slots[2].T
    count = jnp.sum(mk.astype(F32), axis=0, keepdims=True)
    diagonal = jnp.where(sub == lane, count, 0.0).astype(BF)
    cnt = mm(diagonal, ones)

    loads[0].wait()
    pl.semaphore_wait(barrier, len(peers))

    def part_of(table, dz, h):
        wide = table.shape[1] // 2
        return table.at[pl.ds(place_of(dz) * rows, rows), pl.ds(h * wide, wide)]

    def moves(s):
        for way, sign in enumerate((-1, 1)):
            for h in range(2):
                if s < half or h == way:
                    yield way, sign, h

    def ring_start(layer, table, s, halves=(0, 1)):
        for way, sign, h in moves(s):
            if h in halves:
                send(
                    part_of(table, sign * (s - 1), h),
                    part_of(table, sign * s, h),
                    ring_send.at[layer, way, s - 1, h],
                    ring_recv.at[layer, way, s - 1, h],
                    along_z(1 if way == 0 else NZ - 1),
                ).start()

    def ring_wait(layer, table, s, halves=(0, 1)):
        for way, sign, h in moves(s):
            if h in halves:
                drain(part_of(table, sign * s, h), ring_recv.at[layer, way, s - 1, h])

    def ring_pass(layer, table, s):
        for h in range(2):
            ring_wait(layer, table, s, (h,))
            if s < half:
                ring_start(layer, table, s + 1, (h,))

    def ring_left(layer, table):
        for s in range(1, half + 1):
            for way, sign, h in moves(s):
                drain(
                    part_of(table, sign * (s - 1), h), ring_send.at[layer, way, s - 1, h]
                )

    ring_start(0, table1, 1)

    tiles = ncol * block // LANES
    lists[...] = jnp.zeros_like(lists)

    @pl.loop(0, rows // 8)
    def _(i):
        at_rows = pl.ds(pl.multiple_of(i * 8, 8), 8)
        p8 = slot_p[at_rows, :]
        id8 = slot_id[at_rows, :]
        row8 = slot_row[at_rows, :]
        lane8 = iota((8, LANES), 1)
        p_all = [jnp.broadcast_to(p8[:, s : s + 1], (8, LANES)) for s in range(degree)]
        id_all = [jnp.broadcast_to(id8[:, s : s + 1], (8, LANES)) for s in range(degree)]
        for t in range(tiles):
            got = jnp.zeros((8, LANES), jnp.int32)
            for s in range(degree):
                got = jnp.where(p_all[s] == lane8 + t * LANES, id_all[s], got)
            key_ref[at_rows, t * LANES : (t + 1) * LANES] = got
            at_list = t % (tiles // blocks) * blocks + t // (tiles // blocks)
            lists[at_list] = lists[at_list] + jnp.sum(got, axis=0, keepdims=True)
        near = jnp.zeros((8, LANES), F32)
        for s in range(degree):
            near = near + jnp.where(row8[:, s : s + 1] == lane8, 1.0, 0.0)
        loc[at_rows, :] = near

    window = blocks
    for d in range(1, ncol):
        send(
            lists.at[pl.ds(d // 8 * window, window)],
            asked.at[d],
            req_send,
            req_recv,
            behind(d),
        ).start()
    asked[0] = lists[0:window]
    ring_pass(0, table1, 1)

    drain(asked.at[pl.ds(1, ncol - 1)], req_recv)

    reach = []
    for b in range(blocks):
        first, last = b * ROW // CAP, ((b + 1) * ROW - 1) // CAP
        reach.append((first * rows, (last + 1 - first) * rows))

    def pick_block(b):
        first, deep = reach[b]

        @pl.loop(0, ncol)
        def _(d):
            spot = iota((ROW, LANES), 0) + lax.rem(d, 8) * ROW
            piece = jnp.broadcast_to(asked[d, b], (ROW, LANES))
            found = jnp.where(iota((ROW, LANES), 1) == spot, piece, 0)
            found = jnp.sum(found, axis=1, keepdims=True)
            hit = iota((ROW, deep), 1) + (first + 1) == found
            some = pl.ds(pl.multiple_of(d * ROW, ROW), ROW)
            pick[b, some, 0:deep] = one_zero(hit)

    def serve_block(layer, table, serve, b, halves):
        first, deep = reach[b]
        wide = table.shape[1] // 2
        at_col, n_col = halves[0] * wide, len(halves) * wide

        @pl.loop(0, NX)
        def _(j):
            some = pl.ds(pl.multiple_of(j * plane * ROW, plane * ROW), plane * ROW)
            picked = mm(
                pick[b, some, 0:deep],
                table[first : first + deep, at_col : at_col + n_col],
            ).astype(BF)
            serve[b, pl.ds(j * plane, plane), :, at_col : at_col + n_col] = picked.reshape(
                plane, ROW, n_col
            )
            base = lax.rem(me_x + j, NX) * (NZ * NC) + at_z[0]
            for i in range(plane):
                cp = send(
                    serve.at[b, j * plane + i, :, pl.ds(at_col, n_col)],
                    (ans1, ans2)[layer].at[b, j * plane + i, :, pl.ds(at_col, n_col)],
                    ans_send.at[layer, b, halves[0]],
                    ans_recv.at[layer, b, halves[0]],
                    (at_y[i // NC], base + at_c[i % NC]),
                )
                if i == 0:
                    pl.when(j > 0)(cp.start)
                else:
                    cp.start()

    def serve_layer(layer, table, serve, ans):
        if layer == 0:
            pick_block(0)
            serve_block(layer, table, serve, 0, (0, 1))
            ring_pass(layer, table, 2)
            pick_block(1)
            pick_block(2)
        else:
            ring_wait(layer, table, 1, (0,))
            ring_start(layer, table, 2, (0,))
            serve_block(layer, table, serve, 0, (0,))
            ring_wait(layer, table, 1, (1,))
            ring_start(layer, table, 2, (1,))
            serve_block(layer, table, serve, 0, (1,))
            ring_pass(layer, table, 2)
        ring_pass(layer, table, 3)
        serve_block(layer, table, serve, 1, (0, 1))
        ring_pass(layer, table, 4)
        serve_block(layer, table, serve, 2, (0, 1))
        for b in range(blocks):
            ans[b, 0] = serve[b, 0]

    def answers(ref, b, halves):
        wide = ref.shape[3] // 2
        return ref.at[
            b, pl.ds(1, ncol - 1), :, pl.ds(halves[0] * wide, len(halves) * wide)
        ]

    parts = (
        ((0, (0, 1)), (1, (0, 1)), (2, (0, 1))),
        ((0, (0,)), (0, (1,)), (1, (0, 1)), (2, (0, 1))),
    )

    def summed(layer, ans, b, adjacency):
        for part in parts[layer]:
            if part[0] == b:
                drain(answers(ans, *part), ans_recv.at[layer, b, part[1][0]])
        return mm(
            adjacency[:, b * per_block : (b + 1) * per_block],
            ans[b].reshape(per_block, ans.shape[3]),
        )

    serve_layer(0, table1, serve1, ans1)
    pos = pos_ref[...]
    t_dev = pos // rows % n_dev
    t_x = t_dev // (NZ * NC)
    t_z = t_dev // NC % NZ
    target = ((t_x + NX - me_x) % NX) * NZ + (t_z + NZ - me_z) % NZ
    hot_t = iota((NX * NZ, rows), 0) == target
    ahead_of = mm(one_zero(hot_t), sooner)
    rank_t = jnp.sum(jnp.where(hot_t, ahead_of, 0.0), axis=0, keepdims=True)
    move = one_zero(target * rank2 + rank_t.astype(jnp.int32) == sub)
    pos_8 = jnp.broadcast_to((pos % rows).astype(F32), (16, rows)).astype(BF)
    pos_t = lax.dot_general(
        pos_8, move, (((1,), (1,)), ((), ())), preferred_element_type=F32
    )
    pos_out[...] = pos_t[0:8, :]
    for d in range(1, NX * NZ):
        send(pos_out, pos_in.at[d], pos_send, pos_recv, owner_at(d)).start()
    pos_in[0] = pos_out[...]
    adj[...] = one_zero(key_ref[...] > 0)
    adj2[...] = mm(move, adj[...]).astype(BF)
    loc2[...] = mm(move, loc[...].astype(BF))
    cnt2[...] = mm(move, cnt.astype(BF))

    loads[1].wait()
    loads[2].wait()
    x = table1[own, :]
    acc[...] = mm(x, ws1[...])
    total = mm(loc[...].astype(BF), x)
    for b in range(blocks):
        total = total + summed(0, ans1, b, adj)
    m = (total / cnt[:, 0:1]).astype(BF)
    wide = hidden_width // 2
    for h in range(2):
        cols = slice(h * wide, (h + 1) * wide)
        total = acc[:, cols] + mm(m, wn1[:, cols])
        table2[own, cols] = jnp.maximum(total, 0.0).astype(BF)
        ring_start(1, table2, 1, (h,))
    hid[...] = mm(move, table2[own, :]).astype(BF)
    serve_layer(1, table2, serve2, ans2)
    loads[3].wait()
    loads[4].wait()
    acc[...] = mm(hid[...], ws2[...])
    drain(pos_in.at[pl.ds(1, NX * NZ - 1)], pos_recv)
    total = mm(loc2[...].astype(BF), table2[own, :])
    for b in range(blocks):
        total = total + summed(1, ans2, b, adj2)
    m = (total / cnt2[:, 0:1]).astype(BF)
    acc[...] += mm(m, wn2[...])

    fold_rows = 2 * rank2
    pairs = NX * NZ // 2
    low = sub % fold_rows < rank2
    for t in range(n2 // 2):
        a = acc[:, 2 * t * LANES : (2 * t + 1) * LANES]
        b = acc[:, (2 * t + 1) * LANES : (2 * t + 2) * LANES]
        inner = slice(t * fold_rows, (t + 1) * fold_rows)
        first = jnp.where(low, a, pltpu.roll(b, rank2, 0))
        second = jnp.where(low, pltpu.roll(a, rows - rank2, 0), b)
        fold[0:pairs, inner, :] = first.reshape(pairs, fold_rows, LANES)
        fold[pairs:, inner, :] = second.reshape(pairs, fold_rows, LANES)
    leave[...] = fold[...].astype(BF)
    for d in range(1, NX * NZ):
        send(
            leave.at[d % 2 * pairs + d // 2],
            land.at[d % 2 * pairs + d // 2],
            out_send,
            out_recv,
            owner_at(d),
        ).start()
    land[0] = leave[0]

    here = jnp.zeros((1, LANES), F32)
    for d in range(NX * NZ):
        mine_d = iota((1, LANES), 1) // rank2 == d
        here = jnp.where(mine_d, pos_in[d, 0:1, :], here)
    put = one_zero(here == sub.astype(F32))

    drain(land.at[pl.ds(1, 2 * pairs - 1)], out_recv)
    fold[...] = land[...].astype(F32)
    for t in range(n2 // 2):
        inner = slice(t * fold_rows, (t + 1) * fold_rows)
        first = fold[0:pairs, inner, :].reshape(rows, LANES)
        second = fold[pairs:, inner, :].reshape(rows, LANES)
        a = jnp.where(low, first, pltpu.roll(second, rank2, 0))
        b = jnp.where(low, pltpu.roll(first, rows - rank2, 0), second)
        both = jnp.concatenate([a, b], 1).astype(BF)
        out_ref[:, 2 * t * LANES : (2 * t + 2) * LANES] = mm(put, both).astype(BF)

    drain(asked.at[pl.ds(1, ncol - 1)], req_send)
    drain(pos_in.at[pl.ds(1, NX * NZ - 1)], pos_send)
    drain(leave.at[pl.ds(1, 2 * pairs - 1)], out_send)
    for layer, table, serve in ((0, table1, serve1), (1, table2, serve2)):
        ring_left(layer, table)
        for part in parts[layer]:
            drain(answers(serve, *part), ans_send.at[layer, part[0], part[1][0]])


def body(
    features,
    neighbours,
    neighbour_mask,
    layer2_position,
    self_weight1,
    neigh_weight1,
    self_weight2,
    neigh_weight2,
):
    rows, width = features.shape
    hidden = self_weight1.shape[1]
    ny = lax.axis_size("grp")
    ncol = NX * ny * NC
    block = CAP * NZ
    slots = ncol * block
    blocks = block // ROW
    half = NZ // 2
    rank2 = rows // (NX * NZ)
    deep = hidden // LANES * rank2
    vmem = pltpu.VMEM
    dma = pltpu.SemaphoreType.DMA
    return pl.pallas_call(
        kernel,
        out_shape=jax.ShapeDtypeStruct((rows, hidden), BF),
        in_specs=[pl.BlockSpec(memory_space=vmem)] * 3
        + [pl.BlockSpec(memory_space=pl.ANY)] * 5,
        out_specs=pl.BlockSpec(memory_space=vmem),
        scratch_shapes=[
            vmem(self_weight1.shape, BF),
            vmem(neigh_weight1.shape, BF),
            vmem(self_weight2.shape, BF),
            vmem(neigh_weight2.shape, BF),
            vmem((NZ * rows, width), BF),
            vmem((NZ * rows, hidden), BF),
            vmem((blocks, ncol, ROW, width), BF),
            vmem((blocks, ncol, ROW, hidden), BF),
            vmem((blocks, ncol, ROW, width), BF),
            vmem((blocks, ncol, ROW, hidden), BF),
            vmem((blocks, ncol * ROW, 4 * rows), BF),
            vmem((rows, slots), jnp.int32),
            vmem((rows, slots), BF),
            vmem((rows, slots), BF),
            vmem((rows, LANES), F32),
            vmem((rows, LANES), F32),
            vmem((rows, LANES), F32),
            vmem((4, 32, rows), jnp.int32),
            vmem((rows, 32), jnp.int32),
            vmem((rows, 32), jnp.int32),
            vmem((rows, 32), jnp.int32),
            vmem((slots // LANES, 1, LANES), jnp.int32),
            vmem((ncol, blocks, 1, LANES), jnp.int32),
            vmem((rows, hidden), F32),
            vmem((rows, hidden), BF),
            vmem((8, LANES), F32),
            vmem((NX * NZ, 8, LANES), F32),
            vmem((NX * NZ, deep, LANES), F32),
            vmem((NX * NZ, deep, LANES), BF),
            vmem((NX * NZ, deep, LANES), BF),
            dma((5,)),
            dma((2, 2, half, 2)),
            dma((2, 2, half, 2)),
            dma,
            dma,
            dma,
            dma,
            dma((2, blocks, 2)),
            dma((2, blocks, 2)),
            dma,
            dma,
        ],
        compiler_params=pltpu.CompilerParams(
            collective_id=0, has_side_effects=True, vmem_limit_bytes=56 * 2**20
        ),
    )(
        neighbours.T,
        neighbour_mask.T,
        layer2_position.reshape(1, rows),
        features,
        self_weight1,
        neigh_weight1,
        self_weight2,
        neigh_weight2,
    )


def solution(mesh):
    spread = P(("grp", "dev"), None)
    return jax.shard_map(
        body,
        mesh=mesh,
        in_specs=(spread, spread, spread, P(("grp", "dev")), P(), P(), P(), P()),
        out_specs=spread,
        check_vma=False,
    )
```

```python
import jax
import jax.numpy as jnp
from jax import lax
from jax.experimental import pallas as pl
from jax.experimental.pallas import tpu as pltpu
from jax.sharding import PartitionSpec as P

NX, NZ, NC = 4, 8, 2
CAP = 6
LANES = 128
BF = jnp.bfloat16
F32 = jnp.float32
MESH = pl.DeviceIdType.MESH


def iota(shape, dim):
    return lax.broadcasted_iota(jnp.int32, shape, dim)


def mm(a, b):
    return jnp.dot(a, b, preferred_element_type=F32)


def one_zero(cond):
    return jnp.where(cond, 1.0, 0.0).astype(BF)


PLACES = (1, NZ - 1, 0, 2, NZ - 2, 3, NZ - 3, 4)
OWN = PLACES.index(0)
ROW = 16


def place_of(dz):
    return PLACES.index(dz % NZ)


def kernel(
    nb_ref,
    mk_ref,
    pos_ref,
    feat_hbm,
    ws1_hbm,
    wn1_hbm,
    ws2_hbm,
    wn2_hbm,
    out_ref,
    ws1,
    wn1,
    ws2,
    wn2,
    table1,
    table2,
    serve1,
    serve2,
    ans1,
    ans2,
    pick,
    key_ref,
    adj,
    adj2,
    loc,
    loc2,
    cnt2,
    slots,
    slot_p,
    slot_id,
    slot_row,
    lists,
    asked,
    acc,
    hid,
    pos_out,
    pos_in,
    fold,
    leave,
    land,
    load_sem,
    ring_send,
    ring_recv,
    req_send,
    req_recv,
    pos_send,
    pos_recv,
    ans_send,
    ans_recv,
    out_send,
    out_recv,
):
    degree, rows = nb_ref.shape
    ny = lax.axis_size("grp")
    n_dev = NX * NZ * NC
    plane = ny * NC
    ncol = NX * plane
    block = CAP * NZ
    blocks = block // ROW
    per_block = ncol * ROW
    hidden_width = wn2.shape[0]
    n2 = hidden_width // LANES
    half = NZ // 2
    rank2 = rows // (NX * NZ)
    me_y = lax.axis_index("grp")
    me_dev = lax.axis_index("dev")
    me_x = lax.div(me_dev, NZ * NC)
    me_z = lax.rem(lax.div(me_dev, NC), NZ)
    me_c = lax.rem(me_dev, NC)
    at_x = [lax.rem(me_x + k, NX) * (NZ * NC) for k in range(NX)]
    at_y = [lax.rem(me_y + k, ny) for k in range(ny)]
    at_z = [lax.rem(me_z + k, NZ) * NC for k in range(NZ)]
    at_c = [lax.rem(me_c + k, NC) for k in range(NC)]

    def ahead(d):
        return (
            at_y[d // NC % ny],
            at_x[d // plane] + at_z[0] + at_c[d % NC],
        )

    def behind(d):
        return (
            at_y[-(d // NC % ny) % ny],
            at_x[-(d // plane) % NX] + at_z[0] + at_c[-(d % NC) % NC],
        )

    def owner_at(d):
        return (me_y, at_x[d // NZ] + at_z[d % NZ] + me_c)

    def along_z(dz):
        return (me_y, at_x[0] + at_z[dz] + me_c)

    def drain(ref, sem):
        pltpu.make_async_copy(ref, ref, sem).wait()

    def send(src, dst, out, into, device):
        return pltpu.make_async_remote_copy(
            src_ref=src,
            dst_ref=dst,
            send_sem=out,
            recv_sem=into,
            device_id=device,
            device_id_type=MESH,
        )

    own = slice(OWN * rows, (OWN + 1) * rows)

    loads = [
        pltpu.make_async_copy(far, near, load_sem.at[k])
        for k, (far, near) in enumerate(
            (
                (feat_hbm, table1.at[pl.ds(OWN * rows, rows)]),
                (ws1_hbm, ws1),
                (wn1_hbm, wn1),
                (ws2_hbm, ws2),
                (wn2_hbm, wn2),
            )
        )
    ]
    loads[0].start()

    barrier = pltpu.get_barrier_semaphore()
    peers = [along_z(dz) for dz in range(1, NZ)]
    peers += [ahead(d) for d in range(1, ncol)]
    peers += [owner_at(d) for d in range(1, NX * NZ) if d // NZ and d % NZ]
    for peer in peers:
        pl.semaphore_signal(barrier, inc=1, device_id=peer, device_id_type=MESH)
    for load in loads[1:]:
        load.start()

    nb = nb_ref[...]
    mk = mk_ref[...]
    owner = nb // rows
    row = nb % rows
    o_y = owner // n_dev
    o_dev = owner % n_dev
    o_x = o_dev // (NZ * NC)
    o_z = o_dev // NC % NZ
    o_c = o_dev % NC
    mine = owner == me_y * n_dev + me_dev
    valid = mk > 0
    remote = valid & jnp.logical_not(mine)
    col = (
        ((me_x + NX - o_x) % NX) * plane
        + ((me_y + ny - o_y) % ny) * NC
        + (me_c + NC - o_c) % NC
    )
    away = (o_z + NZ - me_z) % NZ
    nearness = jnp.zeros_like(away)
    for k, dz in enumerate(PLACES):
        nearness = jnp.where(away == dz, k, nearness)

    lane = iota((rows, LANES), 1)
    sub = iota((rows, LANES), 0)
    sooner = one_zero(sub < lane)
    ones = jnp.ones((rows, LANES), BF)
    sooner_all = jnp.concatenate([sooner, ones], 1)
    slots[...] = jnp.full_like(slots, -1)
    slots[3, 0:degree, :] = jnp.where(remote, nearness * ncol + col, -1)

    def rank_slot(s, so_far):
        hot = slots[3, pl.ds(s, 1), :] == iota((NZ * ncol, rows), 0)
        counted = mm(one_zero(hot), sooner_all)
        rank = jnp.where(hot, counted[:, :rows] + so_far, 0.0)
        slots[0, pl.ds(s, 1), :] = jnp.sum(rank, axis=0, keepdims=True).astype(jnp.int32)
        return so_far + counted[:, rows:]

    lax.fori_loop(0, degree, rank_slot, jnp.zeros((NZ * ncol, rows), F32))
    spot = nearness * CAP + slots[0, 0:degree, :]
    slots[0, 0:degree, :] = jnp.where(
        remote, spot // ROW * per_block + col * ROW + spot % ROW, -1
    )
    slots[1, 0:degree, :] = nearness * rows + row + 1
    slots[2, 0:degree, :] = jnp.where(valid & mine, row, -1)
    slot_p[...] = slots[0].T
    slot_id[...] = slots[1].T
    slot_row[...] = slots[2].T
    count = jnp.sum(mk.astype(F32), axis=0, keepdims=True)
    diagonal = jnp.where(sub == lane, count, 0.0).astype(BF)
    cnt = mm(diagonal, ones)

    tiles = ncol * block // LANES
    lists[...] = jnp.zeros_like(lists)

    @pl.loop(0, rows // 8)
    def _(i):
        at_rows = pl.ds(pl.multiple_of(i * 8, 8), 8)
        p8 = slot_p[at_rows, :]
        id8 = slot_id[at_rows, :]
        row8 = slot_row[at_rows, :]
        lane8 = iota((8, LANES), 1)
        p_all = [jnp.broadcast_to(p8[:, s : s + 1], (8, LANES)) for s in range(degree)]
        id_all = [jnp.broadcast_to(id8[:, s : s + 1], (8, LANES)) for s in range(degree)]
        for t in range(tiles):
            got = jnp.zeros((8, LANES), jnp.int32)
            for s in range(degree):
                got = jnp.where(p_all[s] == lane8 + t * LANES, id_all[s], got)
            key_ref[at_rows, t * LANES : (t + 1) * LANES] = got
            at_list = t % (tiles // blocks) * blocks + t // (tiles // blocks)
            lists[at_list] = lists[at_list] + jnp.sum(got, axis=0, keepdims=True)
        near = jnp.zeros((8, LANES), F32)
        for s in range(degree):
            near = near + jnp.where(row8[:, s : s + 1] == lane8, 1.0, 0.0)
        loc[at_rows, :] = near

    loads[0].wait()
    pl.semaphore_wait(barrier, len(peers))

    def part_of(table, dz, h):
        wide = table.shape[1] // 2
        return table.at[pl.ds(place_of(dz) * rows, rows), pl.ds(h * wide, wide)]

    def moves(s):
        for way, sign in enumerate((-1, 1)):
            for h in range(2):
                if s < half or h == way:
                    yield way, sign, h

    def ring_start(layer, table, s, halves=(0, 1)):
        for way, sign, h in moves(s):
            if h in halves:
                send(
                    part_of(table, sign * (s - 1), h),
                    part_of(table, sign * s, h),
                    ring_send.at[layer, way, s - 1, h],
                    ring_recv.at[layer, way, s - 1, h],
                    along_z(1 if way == 0 else NZ - 1),
                ).start()

    def ring_wait(layer, table, s, halves=(0, 1)):
        for way, sign, h in moves(s):
            if h in halves:
                drain(part_of(table, sign * s, h), ring_recv.at[layer, way, s - 1, h])

    def ring_pass(layer, table, s):
        for h in range(2):
            ring_wait(layer, table, s, (h,))
            if s < half:
                ring_start(layer, table, s + 1, (h,))

    def ring_left(layer, table):
        for s in range(1, half + 1):
            for way, sign, h in moves(s):
                drain(
                    part_of(table, sign * (s - 1), h), ring_send.at[layer, way, s - 1, h]
                )

    ring_start(0, table1, 1)

    window = blocks
    for d in range(1, ncol):
        send(
            lists.at[pl.ds(d // 8 * window, window)],
            asked.at[d],
            req_send,
            req_recv,
            behind(d),
        ).start()
    asked[0] = lists[0:window]

    drain(asked.at[pl.ds(1, ncol - 1)], req_recv)

    reach = []
    for b in range(blocks):
        first, last = b * ROW // CAP, ((b + 1) * ROW - 1) // CAP
        reach.append((first * rows, (last + 1 - first) * rows))

    def pick_block(b):
        first, deep = reach[b]

        @pl.loop(0, ncol)
        def _(d):
            spot = iota((ROW, LANES), 0) + lax.rem(d, 8) * ROW
            piece = jnp.broadcast_to(asked[d, b], (ROW, LANES))
            found = jnp.where(iota((ROW, LANES), 1) == spot, piece, 0)
            found = jnp.sum(found, axis=1, keepdims=True)
            hit = iota((ROW, deep), 1) + (first + 1) == found
            some = pl.ds(pl.multiple_of(d * ROW, ROW), ROW)
            pick[b, some, 0:deep] = one_zero(hit)

    def serve_block(layer, table, serve, b, halves):
        first, deep = reach[b]
        wide = table.shape[1] // 2
        at_col, n_col = halves[0] * wide, len(halves) * wide

        @pl.loop(0, NX)
        def _(j):
            some = pl.ds(pl.multiple_of(j * plane * ROW, plane * ROW), plane * ROW)
            picked = mm(
                pick[b, some, 0:deep],
                table[first : first + deep, at_col : at_col + n_col],
            ).astype(BF)
            serve[b, pl.ds(j * plane, plane), :, at_col : at_col + n_col] = picked.reshape(
                plane, ROW, n_col
            )
            base = lax.rem(me_x + j, NX) * (NZ * NC) + at_z[0]
            for i in range(plane):
                cp = send(
                    serve.at[b, j * plane + i, :, pl.ds(at_col, n_col)],
                    (ans1, ans2)[layer].at[b, j * plane + i, :, pl.ds(at_col, n_col)],
                    ans_send.at[layer, b, halves[0]],
                    ans_recv.at[layer, b, halves[0]],
                    (at_y[i // NC], base + at_c[i % NC]),
                )
                if i == 0:
                    pl.when(j > 0)(cp.start)
                else:
                    cp.start()

    def serve_layer(layer, table, serve, ans):
        if layer == 0:
            pick_block(0)
        for h in range(2):
            ring_wait(layer, table, 1, (h,))
            ring_start(layer, table, 2, (h,))
            serve_block(layer, table, serve, 0, (h,))
        if layer == 0:
            pick_block(1)
        ring_pass(layer, table, 2)
        if layer == 0:
            pick_block(2)
        ring_pass(layer, table, 3)
        serve_block(layer, table, serve, 1, (0, 1))
        ring_pass(layer, table, 4)
        for h in range(2):
            serve_block(layer, table, serve, 2, (h,))
        for b in range(blocks):
            ans[b, 0] = serve[b, 0]

    def answers(ref, b, halves):
        wide = ref.shape[3] // 2
        return ref.at[
            b, pl.ds(1, ncol - 1), :, pl.ds(halves[0] * wide, len(halves) * wide)
        ]

    parts = ((0, (0,)), (0, (1,)), (1, (0, 1)), (2, (0,)), (2, (1,)))

    def landed_sum(layer, ans, part, adjacency):
        b, halves = part
        wide = ans.shape[3] // 2
        cols = slice(halves[0] * wide, (halves[-1] + 1) * wide)
        drain(answers(ans, b, halves), ans_recv.at[layer, b, halves[0]])
        return mm(
            adjacency[:, b * per_block : (b + 1) * per_block],
            ans[b, :, :, cols].reshape(per_block, len(halves) * wide),
        )

    def means(layer, ans, near, adjacency, degrees):
        wide = ans.shape[3] // 2
        sums = [near[:, h * wide : (h + 1) * wide] for h in range(2)]
        for part in parts:
            got = landed_sum(layer, ans, part, adjacency)
            for k, h in enumerate(part[1]):
                sums[h] = sums[h] + got[:, k * wide : (k + 1) * wide]
            if part[0] == blocks - 1:
                yield slice(h * wide, (h + 1) * wide), (sums[h] / degrees).astype(BF)

    serve_layer(0, table1, serve1, ans1)

    pos = pos_ref[...]
    t_dev = pos // rows % n_dev
    t_x = t_dev // (NZ * NC)
    t_z = t_dev // NC % NZ
    target = ((t_x + NX - me_x) % NX) * NZ + (t_z + NZ - me_z) % NZ
    hot_t = iota((NX * NZ, rows), 0) == target
    ahead_of = mm(one_zero(hot_t), sooner)
    rank_t = jnp.sum(jnp.where(hot_t, ahead_of, 0.0), axis=0, keepdims=True)
    move = one_zero(target * rank2 + rank_t.astype(jnp.int32) == sub)
    pos_8 = jnp.broadcast_to((pos % rows).astype(F32), (16, rows)).astype(BF)
    pos_t = lax.dot_general(
        pos_8, move, (((1,), (1,)), ((), ())), preferred_element_type=F32
    )
    pos_out[...] = pos_t[0:8, :]
    for d in range(1, NX * NZ):
        send(pos_out, pos_in.at[d], pos_send, pos_recv, owner_at(d)).start()
    pos_in[0] = pos_out[...]
    adj[...] = one_zero(key_ref[...] > 0)
    adj2[...] = mm(move, adj[...]).astype(BF)
    loc2[...] = mm(move, loc[...].astype(BF))
    cnt2[...] = mm(move, cnt.astype(BF))

    loads[1].wait()
    loads[2].wait()
    x = table1[own, :]
    acc[...] = mm(x, ws1[...])
    near = mm(loc[...].astype(BF), x)
    halves1 = means(0, ans1, near, adj, cnt[:, 0:1])
    rows_of, m = next(halves1)
    acc[...] += mm(m, wn1[rows_of, :])
    rows_of, m = next(halves1)
    wide = hidden_width // 2
    for h in range(2):
        cols = slice(h * wide, (h + 1) * wide)
        total = acc[:, cols] + mm(m, wn1[rows_of, cols])
        table2[own, cols] = jnp.maximum(total, 0.0).astype(BF)
        ring_start(1, table2, 1, (h,))
    hid[...] = mm(move, table2[own, :]).astype(BF)
    serve_layer(1, table2, serve2, ans2)
    loads[3].wait()
    loads[4].wait()
    acc[...] = mm(hid[...], ws2[...])
    drain(pos_in.at[pl.ds(1, NX * NZ - 1)], pos_recv)
    near = mm(loc2[...].astype(BF), table2[own, :])
    for rows_of, m in means(1, ans2, near, adj2, cnt2[:, 0:1]):
        acc[...] += mm(m, wn2[rows_of, :])

    fold_rows = 2 * rank2
    pairs = NX * NZ // 2
    low = sub % fold_rows < rank2
    for t in range(n2 // 2):
        a = acc[:, 2 * t * LANES : (2 * t + 1) * LANES]
        b = acc[:, (2 * t + 1) * LANES : (2 * t + 2) * LANES]
        inner = slice(t * fold_rows, (t + 1) * fold_rows)
        first = jnp.where(low, a, pltpu.roll(b, rank2, 0))
        second = jnp.where(low, pltpu.roll(a, rows - rank2, 0), b)
        fold[0:pairs, inner, :] = first.reshape(pairs, fold_rows, LANES)
        fold[pairs:, inner, :] = second.reshape(pairs, fold_rows, LANES)
    leave[...] = fold[...].astype(BF)
    for d in range(1, NX * NZ):
        send(
            leave.at[d % 2 * pairs + d // 2],
            land.at[d % 2 * pairs + d // 2],
            out_send,
            out_recv,
            owner_at(d),
        ).start()
    land[0] = leave[0]

    here = jnp.zeros((1, LANES), F32)
    for d in range(NX * NZ):
        mine_d = iota((1, LANES), 1) // rank2 == d
        here = jnp.where(mine_d, pos_in[d, 0:1, :], here)
    put = one_zero(here == sub.astype(F32))

    drain(land.at[pl.ds(1, 2 * pairs - 1)], out_recv)
    fold[...] = land[...].astype(F32)
    for t in range(n2 // 2):
        inner = slice(t * fold_rows, (t + 1) * fold_rows)
        first = fold[0:pairs, inner, :].reshape(rows, LANES)
        second = fold[pairs:, inner, :].reshape(rows, LANES)
        a = jnp.where(low, first, pltpu.roll(second, rank2, 0))
        b = jnp.where(low, pltpu.roll(first, rows - rank2, 0), second)
        both = jnp.concatenate([a, b], 1).astype(BF)
        out_ref[:, 2 * t * LANES : (2 * t + 2) * LANES] = mm(put, both).astype(BF)

    drain(asked.at[pl.ds(1, ncol - 1)], req_send)
    drain(pos_in.at[pl.ds(1, NX * NZ - 1)], pos_send)
    drain(leave.at[pl.ds(1, 2 * pairs - 1)], out_send)
    for layer, table, serve in ((0, table1, serve1), (1, table2, serve2)):
        ring_left(layer, table)
        for part in parts:
            drain(answers(serve, *part), ans_send.at[layer, part[0], part[1][0]])


def body(
    features,
    neighbours,
    neighbour_mask,
    layer2_position,
    self_weight1,
    neigh_weight1,
    self_weight2,
    neigh_weight2,
):
    rows, width = features.shape
    hidden = self_weight1.shape[1]
    ny = lax.axis_size("grp")
    ncol = NX * ny * NC
    block = CAP * NZ
    slots = ncol * block
    blocks = block // ROW
    half = NZ // 2
    rank2 = rows // (NX * NZ)
    deep = hidden // LANES * rank2
    vmem = pltpu.VMEM
    dma = pltpu.SemaphoreType.DMA
    return pl.pallas_call(
        kernel,
        out_shape=jax.ShapeDtypeStruct((rows, hidden), BF),
        in_specs=[pl.BlockSpec(memory_space=vmem)] * 3
        + [pl.BlockSpec(memory_space=pl.ANY)] * 5,
        out_specs=pl.BlockSpec(memory_space=vmem),
        scratch_shapes=[
            vmem(self_weight1.shape, BF),
            vmem(neigh_weight1.shape, BF),
            vmem(self_weight2.shape, BF),
            vmem(neigh_weight2.shape, BF),
            vmem((NZ * rows, width), BF),
            vmem((NZ * rows, hidden), BF),
            vmem((blocks, ncol, ROW, width), BF),
            vmem((blocks, ncol, ROW, hidden), BF),
            vmem((blocks, ncol, ROW, width), BF),
            vmem((blocks, ncol, ROW, hidden), BF),
            vmem((blocks, ncol * ROW, 4 * rows), BF),
            vmem((rows, slots), jnp.int32),
            vmem((rows, slots), BF),
            vmem((rows, slots), BF),
            vmem((rows, LANES), F32),
            vmem((rows, LANES), F32),
            vmem((rows, LANES), F32),
            vmem((4, 32, rows), jnp.int32),
            vmem((rows, 32), jnp.int32),
            vmem((rows, 32), jnp.int32),
            vmem((rows, 32), jnp.int32),
            vmem((slots // LANES, 1, LANES), jnp.int32),
            vmem((ncol, blocks, 1, LANES), jnp.int32),
            vmem((rows, hidden), F32),
            vmem((rows, hidden), BF),
            vmem((8, LANES), F32),
            vmem((NX * NZ, 8, LANES), F32),
            vmem((NX * NZ, deep, LANES), F32),
            vmem((NX * NZ, deep, LANES), BF),
            vmem((NX * NZ, deep, LANES), BF),
            dma((5,)),
            dma((2, 2, half, 2)),
            dma((2, 2, half, 2)),
            dma,
            dma,
            dma,
            dma,
            dma((2, blocks, 2)),
            dma((2, blocks, 2)),
            dma,
            dma,
        ],
        compiler_params=pltpu.CompilerParams(
            collective_id=0, has_side_effects=True, vmem_limit_bytes=56 * 2**20
        ),
    )(
        neighbours.T,
        neighbour_mask.T,
        layer2_position.reshape(1, rows),
        features,
        self_weight1,
        neigh_weight1,
        self_weight2,
        neigh_weight2,
    )


def solution(mesh):
    spread = P(("grp", "dev"), None)
    return jax.shard_map(
        body,
        mesh=mesh,
        in_specs=(spread, spread, spread, P(("grp", "dev")), P(), P(), P(), P()),
        out_specs=spread,
        check_vma=False,
    )
```

```python
import jax
import jax.numpy as jnp
from jax import lax
from jax.experimental import pallas as pl
from jax.experimental.pallas import tpu as pltpu
from jax.sharding import PartitionSpec as P

NX, NZ, NC = 4, 8, 2
CAP = 6
LANES = 128
BF = jnp.bfloat16
F32 = jnp.float32
MESH = pl.DeviceIdType.MESH


def iota(shape, dim):
    return lax.broadcasted_iota(jnp.int32, shape, dim)


def mm(a, b):
    return jnp.dot(a, b, preferred_element_type=F32)


def one_zero(cond):
    return jnp.where(cond, 1.0, 0.0).astype(BF)


PLACES = (1, NZ - 1, 0, 2, NZ - 2, 3, NZ - 3, 4)
OWN = PLACES.index(0)
ROW = 16


def place_of(dz):
    return PLACES.index(dz % NZ)


def kernel(
    nb_ref,
    mk_ref,
    pos_ref,
    feat_hbm,
    ws1_hbm,
    wn1_hbm,
    ws2_hbm,
    wn2_hbm,
    out_ref,
    ws1,
    wn1,
    ws2,
    wn2,
    table1,
    table2,
    serve1,
    serve2,
    ans1,
    ans2,
    pick,
    key_ref,
    adj,
    adj2,
    loc,
    loc2,
    cnt2,
    slots,
    slot_p,
    slot_id,
    slot_row,
    lists,
    asked,
    acc,
    hid,
    pos_out,
    pos_in,
    fold,
    leave,
    land,
    load_sem,
    ring_send,
    ring_recv,
    req_send,
    req_recv,
    pos_send,
    pos_recv,
    ans_send,
    ans_recv,
    out_send,
    out_recv,
):
    degree, rows = nb_ref.shape
    ny = lax.axis_size("grp")
    n_dev = NX * NZ * NC
    plane = ny * NC
    ncol = NX * plane
    block = CAP * NZ
    blocks = block // ROW
    per_block = ncol * ROW
    hidden_width = wn2.shape[0]
    n2 = hidden_width // LANES
    half = NZ // 2
    rank2 = rows // (NX * NZ)
    me_y = lax.axis_index("grp")
    me_dev = lax.axis_index("dev")
    me_x = lax.div(me_dev, NZ * NC)
    me_z = lax.rem(lax.div(me_dev, NC), NZ)
    me_c = lax.rem(me_dev, NC)
    at_x = [lax.rem(me_x + k, NX) * (NZ * NC) for k in range(NX)]
    at_y = [lax.rem(me_y + k, ny) for k in range(ny)]
    at_z = [lax.rem(me_z + k, NZ) * NC for k in range(NZ)]
    at_c = [lax.rem(me_c + k, NC) for k in range(NC)]

    def ahead(d):
        return (
            at_y[d // NC % ny],
            at_x[d // plane] + at_z[0] + at_c[d % NC],
        )

    def behind(d):
        return (
            at_y[-(d // NC % ny) % ny],
            at_x[-(d // plane) % NX] + at_z[0] + at_c[-(d % NC) % NC],
        )

    def owner_at(d):
        return (me_y, at_x[d // NZ] + at_z[d % NZ] + me_c)

    def along_z(dz):
        return (me_y, at_x[0] + at_z[dz] + me_c)

    def drain(ref, sem):
        pltpu.make_async_copy(ref, ref, sem).wait()

    def send(src, dst, out, into, device):
        return pltpu.make_async_remote_copy(
            src_ref=src,
            dst_ref=dst,
            send_sem=out,
            recv_sem=into,
            device_id=device,
            device_id_type=MESH,
        )

    own = slice(OWN * rows, (OWN + 1) * rows)

    loads = [
        pltpu.make_async_copy(far, near, load_sem.at[k])
        for k, (far, near) in enumerate(
            (
                (feat_hbm, table1.at[pl.ds(OWN * rows, rows)]),
                (ws1_hbm, ws1),
                (wn1_hbm, wn1),
                (ws2_hbm, ws2),
                (wn2_hbm, wn2),
            )
        )
    ]
    loads[0].start()

    barrier = pltpu.get_barrier_semaphore()
    peers = [along_z(dz) for dz in range(1, NZ)]
    peers += [ahead(d) for d in range(1, ncol)]
    peers += [owner_at(d) for d in range(1, NX * NZ) if d // NZ and d % NZ]
    for peer in peers:
        pl.semaphore_signal(barrier, inc=1, device_id=peer, device_id_type=MESH)
    for load in loads[1:]:
        load.start()

    nb = nb_ref[...]
    mk = mk_ref[...]
    owner = nb // rows
    row = nb % rows
    o_y = owner // n_dev
    o_dev = owner % n_dev
    o_x = o_dev // (NZ * NC)
    o_z = o_dev // NC % NZ
    o_c = o_dev % NC
    mine = owner == me_y * n_dev + me_dev
    valid = mk > 0
    remote = valid & jnp.logical_not(mine)
    col = (
        ((me_x + NX - o_x) % NX) * plane
        + ((me_y + ny - o_y) % ny) * NC
        + (me_c + NC - o_c) % NC
    )
    away = (o_z + NZ - me_z) % NZ
    nearness = jnp.zeros_like(away)
    for k, dz in enumerate(PLACES):
        nearness = jnp.where(away == dz, k, nearness)

    lane = iota((rows, LANES), 1)
    sub = iota((rows, LANES), 0)
    sooner = one_zero(sub < lane)
    ones = jnp.ones((rows, LANES), BF)
    sooner_all = jnp.concatenate([sooner, ones], 1)
    slots[...] = jnp.full_like(slots, -1)
    slots[3, 0:degree, :] = jnp.where(remote, nearness * ncol + col, -1)

    def rank_slot(s, so_far):
        hot = slots[3, pl.ds(s, 1), :] == iota((NZ * ncol, rows), 0)
        counted = mm(one_zero(hot), sooner_all)
        rank = jnp.where(hot, counted[:, :rows] + so_far, 0.0)
        slots[0, pl.ds(s, 1), :] = jnp.sum(rank, axis=0, keepdims=True).astype(jnp.int32)
        return so_far + counted[:, rows:]

    lax.fori_loop(0, degree, rank_slot, jnp.zeros((NZ * ncol, rows), F32))
    spot = nearness * CAP + slots[0, 0:degree, :]
    slots[0, 0:degree, :] = jnp.where(
        remote, spot // ROW * per_block + col * ROW + spot % ROW, -1
    )
    slots[1, 0:degree, :] = nearness * rows + row + 1
    slots[2, 0:degree, :] = jnp.where(valid & mine, row, -1)
    slot_p[...] = slots[0].T
    slot_id[...] = slots[1].T
    slot_row[...] = slots[2].T
    count = jnp.sum(mk.astype(F32), axis=0, keepdims=True)
    diagonal = jnp.where(sub == lane, count, 0.0).astype(BF)
    cnt = mm(diagonal, ones)

    loads[0].wait()
    pl.semaphore_wait(barrier, len(peers))

    def part_of(table, dz, h):
        wide = table.shape[1] // 2
        return table.at[pl.ds(place_of(dz) * rows, rows), pl.ds(h * wide, wide)]

    def moves(s):
        for way, sign in enumerate((-1, 1)):
            for h in range(2):
                if s < half or h == way:
                    yield way, sign, h

    def ring_start(layer, table, s, halves=(0, 1)):
        for way, sign, h in moves(s):
            if h in halves:
                send(
                    part_of(table, sign * (s - 1), h),
                    part_of(table, sign * s, h),
                    ring_send.at[layer, way, s - 1, h],
                    ring_recv.at[layer, way, s - 1, h],
                    along_z(1 if way == 0 else NZ - 1),
                ).start()

    def ring_wait(layer, table, s, halves=(0, 1)):
        for way, sign, h in moves(s):
            if h in halves:
                drain(part_of(table, sign * s, h), ring_recv.at[layer, way, s - 1, h])

    def ring_pass(layer, table, s):
        for h in range(2):
            ring_wait(layer, table, s, (h,))
            if s < half:
                ring_start(layer, table, s + 1, (h,))

    def ring_left(layer, table):
        for s in range(1, half + 1):
            for way, sign, h in moves(s):
                drain(
                    part_of(table, sign * (s - 1), h), ring_send.at[layer, way, s - 1, h]
                )

    ring_start(0, table1, 1)

    tiles = ncol * block // LANES
    lists[...] = jnp.zeros_like(lists)

    @pl.loop(0, rows // 8)
    def _(i):
        at_rows = pl.ds(pl.multiple_of(i * 8, 8), 8)
        p8 = slot_p[at_rows, :]
        id8 = slot_id[at_rows, :]
        row8 = slot_row[at_rows, :]
        lane8 = iota((8, LANES), 1)
        p_all = [jnp.broadcast_to(p8[:, s : s + 1], (8, LANES)) for s in range(degree)]
        id_all = [jnp.broadcast_to(id8[:, s : s + 1], (8, LANES)) for s in range(degree)]
        for t in range(tiles):
            got = jnp.zeros((8, LANES), jnp.int32)
            for s in range(degree):
                got = jnp.where(p_all[s] == lane8 + t * LANES, id_all[s], got)
            key_ref[at_rows, t * LANES : (t + 1) * LANES] = got
            at_list = t % (tiles // blocks) * blocks + t // (tiles // blocks)
            lists[at_list] = lists[at_list] + jnp.sum(got, axis=0, keepdims=True)
        near = jnp.zeros((8, LANES), F32)
        for s in range(degree):
            near = near + jnp.where(row8[:, s : s + 1] == lane8, 1.0, 0.0)
        loc[at_rows, :] = near

    window = blocks
    for d in range(1, ncol):
        send(
            lists.at[pl.ds(d // 8 * window, window)],
            asked.at[d],
            req_send,
            req_recv,
            behind(d),
        ).start()
    asked[0] = lists[0:window]
    ring_pass(0, table1, 1)

    drain(asked.at[pl.ds(1, ncol - 1)], req_recv)

    reach = []
    for b in range(blocks):
        first, last = b * ROW // CAP, ((b + 1) * ROW - 1) // CAP
        reach.append((first * rows, (last + 1 - first) * rows))

    def pick_block(b):
        first, deep = reach[b]

        @pl.loop(0, ncol)
        def _(d):
            spot = iota((ROW, LANES), 0) + lax.rem(d, 8) * ROW
            piece = jnp.broadcast_to(asked[d, b], (ROW, LANES))
            found = jnp.where(iota((ROW, LANES), 1) == spot, piece, 0)
            found = jnp.sum(found, axis=1, keepdims=True)
            hit = iota((ROW, deep), 1) + (first + 1) == found
            some = pl.ds(pl.multiple_of(d * ROW, ROW), ROW)
            pick[b, some, 0:deep] = one_zero(hit)

    def serve_block(layer, table, serve, b, halves):
        first, deep = reach[b]
        wide = table.shape[1] // 2
        at_col, n_col = halves[0] * wide, len(halves) * wide

        @pl.loop(1, NX + 1)
        def _(turn):
            j = lax.rem(turn, NX)
            some = pl.ds(pl.multiple_of(j * plane * ROW, plane * ROW), plane * ROW)
            picked = mm(
                pick[b, some, 0:deep],
                table[first : first + deep, at_col : at_col + n_col],
            ).astype(BF)
            serve[b, pl.ds(j * plane, plane), :, at_col : at_col + n_col] = picked.reshape(
                plane, ROW, n_col
            )
            base = lax.rem(me_x + j, NX) * (NZ * NC) + at_z[0]
            for i in range(plane):
                cp = send(
                    serve.at[b, j * plane + i, :, pl.ds(at_col, n_col)],
                    (ans1, ans2)[layer].at[b, j * plane + i, :, pl.ds(at_col, n_col)],
                    ans_send.at[layer, b, halves[0]],
                    ans_recv.at[layer, b, halves[0]],
                    (at_y[i // NC], base + at_c[i % NC]),
                )
                if i == 0:
                    pl.when(j > 0)(cp.start)
                else:
                    cp.start()

    def serve_layer(layer, table, serve, ans):
        if layer == 0:
            pick_block(0)
            serve_block(layer, table, serve, 0, (0, 1))
            ring_pass(layer, table, 2)
            pick_block(1)
        else:
            ring_wait(layer, table, 1, (0,))
            ring_start(layer, table, 2, (0,))
            serve_block(layer, table, serve, 0, (0,))
            ring_wait(layer, table, 1, (1,))
            ring_start(layer, table, 2, (1,))
            serve_block(layer, table, serve, 0, (1,))
            ring_pass(layer, table, 2)
        ring_pass(layer, table, 3)
        serve_block(layer, table, serve, 1, (0, 1))
        if layer == 0:
            pick_block(2)
        ring_pass(layer, table, 4)
        serve_block(layer, table, serve, 2, (0, 1))
        for b in range(blocks):
            ans[b, 0] = serve[b, 0]

    def answers(ref, b, halves):
        wide = ref.shape[3] // 2
        return ref.at[
            b, pl.ds(1, ncol - 1), :, pl.ds(halves[0] * wide, len(halves) * wide)
        ]

    parts = (
        ((0, (0, 1)), (1, (0, 1)), (2, (0, 1))),
        ((0, (0,)), (0, (1,)), (1, (0, 1)), (2, (0, 1))),
    )

    def summed(layer, ans, b, adjacency):
        for part in parts[layer]:
            if part[0] == b:
                drain(answers(ans, *part), ans_recv.at[layer, b, part[1][0]])
        return mm(
            adjacency[:, b * per_block : (b + 1) * per_block],
            ans[b].reshape(per_block, ans.shape[3]),
        )

    serve_layer(0, table1, serve1, ans1)
    pos = pos_ref[...]
    t_dev = pos // rows % n_dev
    t_x = t_dev // (NZ * NC)
    t_z = t_dev // NC % NZ
    target = ((t_x + NX - me_x) % NX) * NZ + (t_z + NZ - me_z) % NZ
    hot_t = iota((NX * NZ, rows), 0) == target
    ahead_of = mm(one_zero(hot_t), sooner)
    rank_t = jnp.sum(jnp.where(hot_t, ahead_of, 0.0), axis=0, keepdims=True)
    move = one_zero(target * rank2 + rank_t.astype(jnp.int32) == sub)
    pos_8 = jnp.broadcast_to((pos % rows).astype(F32), (16, rows)).astype(BF)
    pos_t = lax.dot_general(
        pos_8, move, (((1,), (1,)), ((), ())), preferred_element_type=F32
    )
    pos_out[...] = pos_t[0:8, :]
    for d in range(1, NX * NZ):
        send(pos_out, pos_in.at[d], pos_send, pos_recv, owner_at(d)).start()
    pos_in[0] = pos_out[...]
    adj[...] = one_zero(key_ref[...] > 0)
    adj2[...] = mm(move, adj[...]).astype(BF)
    loc2[...] = mm(move, loc[...].astype(BF))
    cnt2[...] = mm(move, cnt.astype(BF))

    loads[1].wait()
    loads[2].wait()
    x = table1[own, :]
    acc[...] = mm(x, ws1[...])
    total = mm(loc[...].astype(BF), x)
    for b in range(blocks):
        total = total + summed(0, ans1, b, adj)
    m = (total / cnt[:, 0:1]).astype(BF)
    wide = hidden_width // 2
    for h in range(2):
        cols = slice(h * wide, (h + 1) * wide)
        total = acc[:, cols] + mm(m, wn1[:, cols])
        table2[own, cols] = jnp.maximum(total, 0.0).astype(BF)
        ring_start(1, table2, 1, (h,))
    hid[...] = mm(move, table2[own, :]).astype(BF)
    serve_layer(1, table2, serve2, ans2)
    loads[3].wait()
    loads[4].wait()
    acc[...] = mm(hid[...], ws2[...])
    drain(pos_in.at[pl.ds(1, NX * NZ - 1)], pos_recv)
    total = mm(loc2[...].astype(BF), table2[own, :])
    for b in range(blocks):
        total = total + summed(1, ans2, b, adj2)
    m = (total / cnt2[:, 0:1]).astype(BF)
    acc[...] += mm(m, wn2[...])

    fold_rows = 2 * rank2
    pairs = NX * NZ // 2
    low = sub % fold_rows < rank2
    for t in range(n2 // 2):
        a = acc[:, 2 * t * LANES : (2 * t + 1) * LANES]
        b = acc[:, (2 * t + 1) * LANES : (2 * t + 2) * LANES]
        inner = slice(t * fold_rows, (t + 1) * fold_rows)
        first = jnp.where(low, a, pltpu.roll(b, rank2, 0))
        second = jnp.where(low, pltpu.roll(a, rows - rank2, 0), b)
        fold[0:pairs, inner, :] = first.reshape(pairs, fold_rows, LANES)
        fold[pairs:, inner, :] = second.reshape(pairs, fold_rows, LANES)
    leave[...] = fold[...].astype(BF)
    for d in range(1, NX * NZ):
        send(
            leave.at[d % 2 * pairs + d // 2],
            land.at[d % 2 * pairs + d // 2],
            out_send,
            out_recv,
            owner_at(d),
        ).start()
    land[0] = leave[0]

    here = jnp.zeros((1, LANES), F32)
    for d in range(NX * NZ):
        mine_d = iota((1, LANES), 1) // rank2 == d
        here = jnp.where(mine_d, pos_in[d, 0:1, :], here)
    put = one_zero(here == sub.astype(F32))

    drain(land.at[pl.ds(1, 2 * pairs - 1)], out_recv)
    fold[...] = land[...].astype(F32)
    for t in range(n2 // 2):
        inner = slice(t * fold_rows, (t + 1) * fold_rows)
        first = fold[0:pairs, inner, :].reshape(rows, LANES)
        second = fold[pairs:, inner, :].reshape(rows, LANES)
        a = jnp.where(low, first, pltpu.roll(second, rank2, 0))
        b = jnp.where(low, pltpu.roll(first, rows - rank2, 0), second)
        both = jnp.concatenate([a, b], 1).astype(BF)
        out_ref[:, 2 * t * LANES : (2 * t + 2) * LANES] = mm(put, both).astype(BF)

    drain(asked.at[pl.ds(1, ncol - 1)], req_send)
    drain(pos_in.at[pl.ds(1, NX * NZ - 1)], pos_send)
    drain(leave.at[pl.ds(1, 2 * pairs - 1)], out_send)
    for layer, table, serve in ((0, table1, serve1), (1, table2, serve2)):
        ring_left(layer, table)
        for part in parts[layer]:
            drain(answers(serve, *part), ans_send.at[layer, part[0], part[1][0]])


def body(
    features,
    neighbours,
    neighbour_mask,
    layer2_position,
    self_weight1,
    neigh_weight1,
    self_weight2,
    neigh_weight2,
):
    rows, width = features.shape
    hidden = self_weight1.shape[1]
    ny = lax.axis_size("grp")
    ncol = NX * ny * NC
    block = CAP * NZ
    slots = ncol * block
    blocks = block // ROW
    half = NZ // 2
    rank2 = rows // (NX * NZ)
    deep = hidden // LANES * rank2
    vmem = pltpu.VMEM
    dma = pltpu.SemaphoreType.DMA
    return pl.pallas_call(
        kernel,
        out_shape=jax.ShapeDtypeStruct((rows, hidden), BF),
        in_specs=[pl.BlockSpec(memory_space=vmem)] * 3
        + [pl.BlockSpec(memory_space=pl.ANY)] * 5,
        out_specs=pl.BlockSpec(memory_space=vmem),
        scratch_shapes=[
            vmem(self_weight1.shape, BF),
            vmem(neigh_weight1.shape, BF),
            vmem(self_weight2.shape, BF),
            vmem(neigh_weight2.shape, BF),
            vmem((NZ * rows, width), BF),
            vmem((NZ * rows, hidden), BF),
            vmem((blocks, ncol, ROW, width), BF),
            vmem((blocks, ncol, ROW, hidden), BF),
            vmem((blocks, ncol, ROW, width), BF),
            vmem((blocks, ncol, ROW, hidden), BF),
            vmem((blocks, ncol * ROW, 4 * rows), BF),
            vmem((rows, slots), jnp.int32),
            vmem((rows, slots), BF),
            vmem((rows, slots), BF),
            vmem((rows, LANES), F32),
            vmem((rows, LANES), F32),
            vmem((rows, LANES), F32),
            vmem((4, 32, rows), jnp.int32),
            vmem((rows, 32), jnp.int32),
            vmem((rows, 32), jnp.int32),
            vmem((rows, 32), jnp.int32),
            vmem((slots // LANES, 1, LANES), jnp.int32),
            vmem((ncol, blocks, 1, LANES), jnp.int32),
            vmem((rows, hidden), F32),
            vmem((rows, hidden), BF),
            vmem((8, LANES), F32),
            vmem((NX * NZ, 8, LANES), F32),
            vmem((NX * NZ, deep, LANES), F32),
            vmem((NX * NZ, deep, LANES), BF),
            vmem((NX * NZ, deep, LANES), BF),
            dma((5,)),
            dma((2, 2, half, 2)),
            dma((2, 2, half, 2)),
            dma,
            dma,
            dma,
            dma,
            dma((2, blocks, 2)),
            dma((2, blocks, 2)),
            dma,
            dma,
        ],
        compiler_params=pltpu.CompilerParams(
            collective_id=0, has_side_effects=True, vmem_limit_bytes=56 * 2**20
        ),
    )(
        neighbours.T,
        neighbour_mask.T,
        layer2_position.reshape(1, rows),
        features,
        self_weight1,
        neigh_weight1,
        self_weight2,
        neigh_weight2,
    )


def solution(mesh):
    spread = P(("grp", "dev"), None)
    return jax.shard_map(
        body,
        mesh=mesh,
        in_specs=(spread, spread, spread, P(("grp", "dev")), P(), P(), P(), P()),
        out_specs=spread,
        check_vma=False,
    )
```

```python
import jax
import jax.numpy as jnp
from jax import lax
from jax.experimental import pallas as pl
from jax.experimental.pallas import tpu as pltpu
from jax.sharding import PartitionSpec as P

NX, NZ, NC = 4, 8, 2
CAP = 6
LANES = 128
BF = jnp.bfloat16
F32 = jnp.float32
MESH = pl.DeviceIdType.MESH


def iota(shape, dim):
    return lax.broadcasted_iota(jnp.int32, shape, dim)


def mm(a, b):
    return jnp.dot(a, b, preferred_element_type=F32)


def one_zero(cond):
    return jnp.where(cond, 1.0, 0.0).astype(BF)


PLACES = (1, NZ - 1, 0, 2, NZ - 2, 3, NZ - 3, 4)
OWN = PLACES.index(0)
ROW = 16


def place_of(dz):
    return PLACES.index(dz % NZ)


def kernel(
    nb_ref,
    mk_ref,
    pos_ref,
    feat_hbm,
    ws1_hbm,
    wn1_hbm,
    ws2_hbm,
    wn2_hbm,
    out_ref,
    ws1,
    wn1,
    ws2,
    wn2,
    table1,
    table2,
    serve1,
    serve2,
    ans1,
    ans2,
    pick,
    key_ref,
    adj,
    adj2,
    loc,
    loc2,
    cnt2,
    slots,
    slot_p,
    slot_id,
    slot_row,
    lists,
    asked,
    acc,
    hid,
    pos_out,
    pos_in,
    fold,
    leave,
    land,
    load_sem,
    ring_send,
    ring_recv,
    req_send,
    req_recv,
    pos_send,
    pos_recv,
    ans_send,
    ans_recv,
    out_send,
    out_recv,
):
    degree, rows = nb_ref.shape
    ny = lax.axis_size("grp")
    n_dev = NX * NZ * NC
    plane = ny * NC
    ncol = NX * plane
    block = CAP * NZ
    blocks = block // ROW
    per_block = ncol * ROW
    hidden_width = wn2.shape[0]
    n2 = hidden_width // LANES
    half = NZ // 2
    rank2 = rows // (NX * NZ)
    me_y = lax.axis_index("grp")
    me_dev = lax.axis_index("dev")
    me_x = lax.div(me_dev, NZ * NC)
    me_z = lax.rem(lax.div(me_dev, NC), NZ)
    me_c = lax.rem(me_dev, NC)
    at_x = [lax.rem(me_x + k, NX) * (NZ * NC) for k in range(NX)]
    at_y = [lax.rem(me_y + k, ny) for k in range(ny)]
    at_z = [lax.rem(me_z + k, NZ) * NC for k in range(NZ)]
    at_c = [lax.rem(me_c + k, NC) for k in range(NC)]

    def ahead(d):
        return (
            at_y[d // NC % ny],
            at_x[d // plane] + at_z[0] + at_c[d % NC],
        )

    def behind(d):
        return (
            at_y[-(d // NC % ny) % ny],
            at_x[-(d // plane) % NX] + at_z[0] + at_c[-(d % NC) % NC],
        )

    def owner_at(d):
        return (me_y, at_x[d // NZ] + at_z[d % NZ] + me_c)

    def along_z(dz):
        return (me_y, at_x[0] + at_z[dz] + me_c)

    def drain(ref, sem):
        pltpu.make_async_copy(ref, ref, sem).wait()

    def send(src, dst, out, into, device):
        return pltpu.make_async_remote_copy(
            src_ref=src,
            dst_ref=dst,
            send_sem=out,
            recv_sem=into,
            device_id=device,
            device_id_type=MESH,
        )

    own = slice(OWN * rows, (OWN + 1) * rows)

    loads = [
        pltpu.make_async_copy(far, near, load_sem.at[k])
        for k, (far, near) in enumerate(
            (
                (feat_hbm, table1.at[pl.ds(OWN * rows, rows)]),
                (ws1_hbm, ws1),
                (wn1_hbm, wn1),
                (ws2_hbm, ws2),
                (wn2_hbm, wn2),
            )
        )
    ]
    loads[0].start()

    barrier = pltpu.get_barrier_semaphore()
    peers = [along_z(dz) for dz in range(1, NZ)]
    peers += [ahead(d) for d in range(1, ncol)]
    peers += [owner_at(d) for d in range(1, NX * NZ) if d // NZ and d % NZ]
    for peer in peers:
        pl.semaphore_signal(barrier, inc=1, device_id=peer, device_id_type=MESH)
    for load in loads[1:]:
        load.start()

    nb = nb_ref[...]
    mk = mk_ref[...]
    owner = nb // rows
    row = nb % rows
    o_y = owner // n_dev
    o_dev = owner % n_dev
    o_x = o_dev // (NZ * NC)
    o_z = o_dev // NC % NZ
    o_c = o_dev % NC
    mine = owner == me_y * n_dev + me_dev
    valid = mk > 0
    remote = valid & jnp.logical_not(mine)
    col = (
        ((me_x + NX - o_x) % NX) * plane
        + ((me_y + ny - o_y) % ny) * NC
        + (me_c + NC - o_c) % NC
    )
    away = (o_z + NZ - me_z) % NZ
    nearness = jnp.zeros_like(away)
    for k, dz in enumerate(PLACES):
        nearness = jnp.where(away == dz, k, nearness)

    lane = iota((rows, LANES), 1)
    sub = iota((rows, LANES), 0)
    sooner = one_zero(sub < lane)
    ones = jnp.ones((rows, LANES), BF)
    sooner_all = jnp.concatenate([sooner, ones], 1)
    slots[...] = jnp.full_like(slots, -1)
    slots[3, 0:degree, :] = jnp.where(remote, nearness * ncol + col, -1)

    def rank_slot(s, so_far):
        hot = slots[3, pl.ds(s, 1), :] == iota((NZ * ncol, rows), 0)
        counted = mm(one_zero(hot), sooner_all)
        rank = jnp.where(hot, counted[:, :rows] + so_far, 0.0)
        slots[0, pl.ds(s, 1), :] = jnp.sum(rank, axis=0, keepdims=True).astype(jnp.int32)
        return so_far + counted[:, rows:]

    lax.fori_loop(0, degree, rank_slot, jnp.zeros((NZ * ncol, rows), F32))
    spot = nearness * CAP + slots[0, 0:degree, :]
    slots[0, 0:degree, :] = jnp.where(
        remote, spot // ROW * per_block + col * ROW + spot % ROW, -1
    )
    slots[1, 0:degree, :] = nearness * rows + row + 1
    slots[2, 0:degree, :] = jnp.where(valid & mine, row, -1)
    slot_p[...] = slots[0].T
    slot_id[...] = slots[1].T
    slot_row[...] = slots[2].T
    count = jnp.sum(mk.astype(F32), axis=0, keepdims=True)
    diagonal = jnp.where(sub == lane, count, 0.0).astype(BF)
    cnt = mm(diagonal, ones)

    loads[0].wait()
    pl.semaphore_wait(barrier, len(peers))

    def part_of(table, dz, h):
        wide = table.shape[1] // 2
        return table.at[pl.ds(place_of(dz) * rows, rows), pl.ds(h * wide, wide)]

    def moves(s):
        for way, sign in enumerate((-1, 1)):
            for h in range(2):
                if s < half or h == way:
                    yield way, sign, h

    def ring_start(layer, table, s, halves=(0, 1)):
        for way, sign, h in moves(s):
            if h in halves:
                send(
                    part_of(table, sign * (s - 1), h),
                    part_of(table, sign * s, h),
                    ring_send.at[layer, way, s - 1, h],
                    ring_recv.at[layer, way, s - 1, h],
                    along_z(1 if way == 0 else NZ - 1),
                ).start()

    def ring_wait(layer, table, s, halves=(0, 1)):
        for way, sign, h in moves(s):
            if h in halves:
                drain(part_of(table, sign * s, h), ring_recv.at[layer, way, s - 1, h])

    def ring_pass(layer, table, s):
        for h in range(2):
            ring_wait(layer, table, s, (h,))
            if s < half:
                ring_start(layer, table, s + 1, (h,))

    def ring_left(layer, table):
        for s in range(1, half + 1):
            for way, sign, h in moves(s):
                drain(
                    part_of(table, sign * (s - 1), h), ring_send.at[layer, way, s - 1, h]
                )

    ring_start(0, table1, 1)

    tiles = ncol * block // LANES
    lists[...] = jnp.zeros_like(lists)

    @pl.loop(0, rows // 8)
    def _(i):
        at_rows = pl.ds(pl.multiple_of(i * 8, 8), 8)
        p8 = slot_p[at_rows, :]
        id8 = slot_id[at_rows, :]
        row8 = slot_row[at_rows, :]
        lane8 = iota((8, LANES), 1)
        p_all = [jnp.broadcast_to(p8[:, s : s + 1], (8, LANES)) for s in range(degree)]
        id_all = [jnp.broadcast_to(id8[:, s : s + 1], (8, LANES)) for s in range(degree)]
        for t in range(tiles):
            got = jnp.zeros((8, LANES), jnp.int32)
            for s in range(degree):
                got = jnp.where(p_all[s] == lane8 + t * LANES, id_all[s], got)
            key_ref[at_rows, t * LANES : (t + 1) * LANES] = got
            at_list = t % (tiles // blocks) * blocks + t // (tiles // blocks)
            lists[at_list] = lists[at_list] + jnp.sum(got, axis=0, keepdims=True)
        near = jnp.zeros((8, LANES), F32)
        for s in range(degree):
            near = near + jnp.where(row8[:, s : s + 1] == lane8, 1.0, 0.0)
        loc[at_rows, :] = near

    window = blocks
    for d in range(1, ncol):
        send(
            lists.at[pl.ds(d // 8 * window, window)],
            asked.at[d],
            req_send,
            req_recv,
            behind(d),
        ).start()
    asked[0] = lists[0:window]
    ring_pass(0, table1, 1)

    drain(asked.at[pl.ds(1, ncol - 1)], req_recv)

    reach = []
    for b in range(blocks):
        first, last = b * ROW // CAP, ((b + 1) * ROW - 1) // CAP
        reach.append((first * rows, (last + 1 - first) * rows))

    def pick_block(b):
        first, deep = reach[b]

        @pl.loop(0, ncol)
        def _(d):
            spot = iota((ROW, LANES), 0) + lax.rem(d, 8) * ROW
            piece = jnp.broadcast_to(asked[d, b], (ROW, LANES))
            found = jnp.where(iota((ROW, LANES), 1) == spot, piece, 0)
            found = jnp.sum(found, axis=1, keepdims=True)
            hit = iota((ROW, deep), 1) + (first + 1) == found
            some = pl.ds(pl.multiple_of(d * ROW, ROW), ROW)
            pick[b, some, 0:deep] = one_zero(hit)

    def serve_block(layer, table, serve, b, halves):
        first, deep = reach[b]
        wide = table.shape[1] // 2
        at_col, n_col = halves[0] * wide, len(halves) * wide

        @pl.loop(1, NX + 1)
        def _(turn):
            j = lax.rem(turn, NX)
            some = pl.ds(pl.multiple_of(j * plane * ROW, plane * ROW), plane * ROW)
            picked = mm(
                pick[b, some, 0:deep],
                table[first : first + deep, at_col : at_col + n_col],
            ).astype(BF)
            serve[b, pl.ds(j * plane, plane), :, at_col : at_col + n_col] = picked.reshape(
                plane, ROW, n_col
            )
            base = lax.rem(me_x + j, NX) * (NZ * NC) + at_z[0]
            for i in range(plane):
                cp = send(
                    serve.at[b, j * plane + i, :, pl.ds(at_col, n_col)],
                    (ans1, ans2)[layer].at[b, j * plane + i, :, pl.ds(at_col, n_col)],
                    ans_send.at[layer, b, halves[0]],
                    ans_recv.at[layer, b, halves[0]],
                    (at_y[i // NC], base + at_c[i % NC]),
                )
                if i == 0:
                    pl.when(j > 0)(cp.start)
                else:
                    cp.start()

    def serve_layer(layer, table, serve, ans):
        if layer == 0:
            pick_block(0)
            ring_pass(layer, table, 2)
            serve_block(layer, table, serve, 0, (0, 1))
            pick_block(1)
        else:
            ring_wait(layer, table, 1, (0,))
            ring_start(layer, table, 2, (0,))
            serve_block(layer, table, serve, 0, (0,))
            ring_wait(layer, table, 1, (1,))
            ring_start(layer, table, 2, (1,))
            serve_block(layer, table, serve, 0, (1,))
            ring_pass(layer, table, 2)
        ring_pass(layer, table, 3)
        serve_block(layer, table, serve, 1, (0, 1))
        if layer == 0:
            pick_block(2)
        ring_pass(layer, table, 4)
        serve_block(layer, table, serve, 2, (0, 1))
        for b in range(blocks):
            ans[b, 0] = serve[b, 0]

    def answers(ref, b, halves):
        wide = ref.shape[3] // 2
        return ref.at[
            b, pl.ds(1, ncol - 1), :, pl.ds(halves[0] * wide, len(halves) * wide)
        ]

    parts = (
        ((0, (0, 1)), (1, (0, 1)), (2, (0, 1))),
        ((0, (0,)), (0, (1,)), (1, (0, 1)), (2, (0, 1))),
    )

    def summed(layer, ans, b, adjacency):
        for part in parts[layer]:
            if part[0] == b:
                drain(answers(ans, *part), ans_recv.at[layer, b, part[1][0]])
        return mm(
            adjacency[:, b * per_block : (b + 1) * per_block],
            ans[b].reshape(per_block, ans.shape[3]),
        )

    serve_layer(0, table1, serve1, ans1)
    pos = pos_ref[...]
    t_dev = pos // rows % n_dev
    t_x = t_dev // (NZ * NC)
    t_z = t_dev // NC % NZ
    target = ((t_x + NX - me_x) % NX) * NZ + (t_z + NZ - me_z) % NZ
    hot_t = iota((NX * NZ, rows), 0) == target
    ahead_of = mm(one_zero(hot_t), sooner)
    rank_t = jnp.sum(jnp.where(hot_t, ahead_of, 0.0), axis=0, keepdims=True)
    move = one_zero(target * rank2 + rank_t.astype(jnp.int32) == sub)
    pos_8 = jnp.broadcast_to((pos % rows).astype(F32), (16, rows)).astype(BF)
    pos_t = lax.dot_general(
        pos_8, move, (((1,), (1,)), ((), ())), preferred_element_type=F32
    )
    pos_out[...] = pos_t[0:8, :]
    for d in range(1, NX * NZ):
        send(pos_out, pos_in.at[d], pos_send, pos_recv, owner_at(d)).start()
    pos_in[0] = pos_out[...]
    adj[...] = one_zero(key_ref[...] > 0)
    adj2[...] = mm(move, adj[...]).astype(BF)
    loc2[...] = mm(move, loc[...].astype(BF))
    cnt2[...] = mm(move, cnt.astype(BF))

    loads[1].wait()
    loads[2].wait()
    x = table1[own, :]
    acc[...] = mm(x, ws1[...])
    total = mm(loc[...].astype(BF), x)
    for b in range(blocks):
        total = total + summed(0, ans1, b, adj)
    m = (total / cnt[:, 0:1]).astype(BF)
    wide = hidden_width // 2
    for h in range(2):
        cols = slice(h * wide, (h + 1) * wide)
        total = acc[:, cols] + mm(m, wn1[:, cols])
        table2[own, cols] = jnp.maximum(total, 0.0).astype(BF)
        ring_start(1, table2, 1, (h,))
    hid[...] = mm(move, table2[own, :]).astype(BF)
    serve_layer(1, table2, serve2, ans2)
    loads[3].wait()
    loads[4].wait()
    acc[...] = mm(hid[...], ws2[...])
    drain(pos_in.at[pl.ds(1, NX * NZ - 1)], pos_recv)
    total = mm(loc2[...].astype(BF), table2[own, :])
    for b in range(blocks):
        total = total + summed(1, ans2, b, adj2)
    m = (total / cnt2[:, 0:1]).astype(BF)
    acc[...] += mm(m, wn2[...])

    fold_rows = 2 * rank2
    pairs = NX * NZ // 2
    low = sub % fold_rows < rank2
    for t in range(n2 // 2):
        a = acc[:, 2 * t * LANES : (2 * t + 1) * LANES]
        b = acc[:, (2 * t + 1) * LANES : (2 * t + 2) * LANES]
        inner = slice(t * fold_rows, (t + 1) * fold_rows)
        first = jnp.where(low, a, pltpu.roll(b, rank2, 0))
        second = jnp.where(low, pltpu.roll(a, rows - rank2, 0), b)
        fold[0:pairs, inner, :] = first.reshape(pairs, fold_rows, LANES)
        fold[pairs:, inner, :] = second.reshape(pairs, fold_rows, LANES)
    leave[...] = fold[...].astype(BF)
    for d in range(1, NX * NZ):
        send(
            leave.at[d % 2 * pairs + d // 2],
            land.at[d % 2 * pairs + d // 2],
            out_send,
            out_recv,
            owner_at(d),
        ).start()
    land[0] = leave[0]

    here = jnp.zeros((1, LANES), F32)
    for d in range(NX * NZ):
        mine_d = iota((1, LANES), 1) // rank2 == d
        here = jnp.where(mine_d, pos_in[d, 0:1, :], here)
    put = one_zero(here == sub.astype(F32))

    drain(land.at[pl.ds(1, 2 * pairs - 1)], out_recv)
    fold[...] = land[...].astype(F32)
    for t in range(n2 // 2):
        inner = slice(t * fold_rows, (t + 1) * fold_rows)
        first = fold[0:pairs, inner, :].reshape(rows, LANES)
        second = fold[pairs:, inner, :].reshape(rows, LANES)
        a = jnp.where(low, first, pltpu.roll(second, rank2, 0))
        b = jnp.where(low, pltpu.roll(first, rows - rank2, 0), second)
        both = jnp.concatenate([a, b], 1).astype(BF)
        out_ref[:, 2 * t * LANES : (2 * t + 2) * LANES] = mm(put, both).astype(BF)

    drain(asked.at[pl.ds(1, ncol - 1)], req_send)
    drain(pos_in.at[pl.ds(1, NX * NZ - 1)], pos_send)
    drain(leave.at[pl.ds(1, 2 * pairs - 1)], out_send)
    for layer, table, serve in ((0, table1, serve1), (1, table2, serve2)):
        ring_left(layer, table)
        for part in parts[layer]:
            drain(answers(serve, *part), ans_send.at[layer, part[0], part[1][0]])


def body(
    features,
    neighbours,
    neighbour_mask,
    layer2_position,
    self_weight1,
    neigh_weight1,
    self_weight2,
    neigh_weight2,
):
    rows, width = features.shape
    hidden = self_weight1.shape[1]
    ny = lax.axis_size("grp")
    ncol = NX * ny * NC
    block = CAP * NZ
    slots = ncol * block
    blocks = block // ROW
    half = NZ // 2
    rank2 = rows // (NX * NZ)
    deep = hidden // LANES * rank2
    vmem = pltpu.VMEM
    dma = pltpu.SemaphoreType.DMA
    return pl.pallas_call(
        kernel,
        out_shape=jax.ShapeDtypeStruct((rows, hidden), BF),
        in_specs=[pl.BlockSpec(memory_space=vmem)] * 3
        + [pl.BlockSpec(memory_space=pl.ANY)] * 5,
        out_specs=pl.BlockSpec(memory_space=vmem),
        scratch_shapes=[
            vmem(self_weight1.shape, BF),
            vmem(neigh_weight1.shape, BF),
            vmem(self_weight2.shape, BF),
            vmem(neigh_weight2.shape, BF),
            vmem((NZ * rows, width), BF),
            vmem((NZ * rows, hidden), BF),
            vmem((blocks, ncol, ROW, width), BF),
            vmem((blocks, ncol, ROW, hidden), BF),
            vmem((blocks, ncol, ROW, width), BF),
            vmem((blocks, ncol, ROW, hidden), BF),
            vmem((blocks, ncol * ROW, 4 * rows), BF),
            vmem((rows, slots), jnp.int32),
            vmem((rows, slots), BF),
            vmem((rows, slots), BF),
            vmem((rows, LANES), F32),
            vmem((rows, LANES), F32),
            vmem((rows, LANES), F32),
            vmem((4, 32, rows), jnp.int32),
            vmem((rows, 32), jnp.int32),
            vmem((rows, 32), jnp.int32),
            vmem((rows, 32), jnp.int32),
            vmem((slots // LANES, 1, LANES), jnp.int32),
            vmem((ncol, blocks, 1, LANES), jnp.int32),
            vmem((rows, hidden), F32),
            vmem((rows, hidden), BF),
            vmem((8, LANES), F32),
            vmem((NX * NZ, 8, LANES), F32),
            vmem((NX * NZ, deep, LANES), F32),
            vmem((NX * NZ, deep, LANES), BF),
            vmem((NX * NZ, deep, LANES), BF),
            dma((5,)),
            dma((2, 2, half, 2)),
            dma((2, 2, half, 2)),
            dma,
            dma,
            dma,
            dma,
            dma((2, blocks, 2)),
            dma((2, blocks, 2)),
            dma,
            dma,
        ],
        compiler_params=pltpu.CompilerParams(
            collective_id=0, has_side_effects=True, vmem_limit_bytes=56 * 2**20
        ),
    )(
        neighbours.T,
        neighbour_mask.T,
        layer2_position.reshape(1, rows),
        features,
        self_weight1,
        neigh_weight1,
        self_weight2,
        neigh_weight2,
    )


def solution(mesh):
    spread = P(("grp", "dev"), None)
    return jax.shard_map(
        body,
        mesh=mesh,
        in_specs=(spread, spread, spread, P(("grp", "dev")), P(), P(), P(), P()),
        out_specs=spread,
        check_vma=False,
    )
```
